256 devices in a mesh: freq: 8 (over z_lo, y), slab: 32 (over z_hi, x, core).
Axes of the slice: x: 4, y: 4, z: 8 (z_hi: 4, z_lo: 2; z = z_hi * 2 + z_lo), core: 2. Of those that a mesh axis runs over, the one named last changes fastest.
Arguments:
- wavefield: float32 [2, 8, 2048, 2048], P(None, 'freq', 'slab'), may hold values from -6 to 6
- freqs: float32 [8], P('freq'), may hold values from 0.15 to 0.45
- velocity: float32 [3, 2048, 2048], P(None, 'slab', 'freq'), may hold values from 0.7 to 1.6
- ref_slow: float32 [3, 2], replicated, may hold values from 0.6 to 1.5, as said below
Outputs:
- migrated: float32 [2, 8, 2048, 2048], P(None, 'freq', 'slab')
The draws below stay inside these ranges and needn't reach their ends.
Inputs may be any that keep to these rules, and one draw needn't show every extreme that they name: ref_slow[d, 1] - ref_slow[d, 0] lies between 0.3 and 0.6 for every depth step.
All inputs are finite; a program needn't handle non-finite values.
Results may differ from the reference program's by a relative error of at most 0.0003.
Values sent between devices are 32-bit elements; how exact they have to be, the bound alone decides.
No kernel may reach another device: no remote copies, remote signals or barrier semaphores. Data moves between devices by JAX's collectives and lax.ppermute only.
A program may use at most 64 MiB of HBM per device.

```python
import math
import jax
import jax.numpy as jnp
from jax import lax

NX = 2048
NY = 2048
DEPTH = 3
FREQ = 8


def draw_ref_slow(key, part):
    first_key, second_key = jax.random.split(jax.random.fold_in(key, 11))
    lower = jax.random.uniform(first_key, (DEPTH,), jnp.float32, 0.6, 0.9)
    spacing = jax.random.uniform(second_key, (DEPTH,), jnp.float32, 0.3, 0.6)
    return jnp.stack([lower, lower + spacing], axis=1)


def block_levels(rng, extent, cuts, smallest, largest):
    def one(dim, parts):
        steps = jax.random.uniform(jax.random.fold_in(jax.random.fold_in(rng, 6), dim), (parts,), jnp.float32, smallest / len(cuts), largest / len(cuts))
        return jnp.repeat(jnp.exp(steps), extent[dim] // parts).reshape((-1,) + (1,) * (len(extent) - dim - 1))

    loudness = one(*cuts[0])
    for cut in cuts[1:]:
        loudness = loudness * one(*cut)
    return loudness


def bell_draw(rng, extent, deviation, bound, cuts=(), kind=jnp.bfloat16):
    factor_of = block_levels(rng, extent, cuts, -0.22, 0.18) if cuts else 1.0
    values = jax.random.normal(rng, extent, jnp.float32) * deviation * factor_of
    return jnp.minimum(jnp.maximum(values, -bound), bound).astype(kind)


def setup_inputs(seed: int = 0) -> dict:
    splits = jax.random.split(jax.random.key(seed), 5)
    return {
        "wavefield": bell_draw(splits[0], (2, FREQ, NX, NY), 1.0, 6.0, ((1, 8), (2, 32)), jnp.float32),
        "freqs": jnp.clip(0.15 + 0.29999998 * jax.random.uniform(splits[1], (FREQ,), jnp.float32) ** block_levels(splits[1], (FREQ,), ((0, 8),), -0.2, 0.2), 0.15, 0.45),
        "velocity": jnp.clip(0.7 + 0.90000004 * jax.random.uniform(splits[2], (DEPTH, NX, NY), jnp.float32) ** block_levels(splits[2], (DEPTH, NX, NY), ((1, 32), (2, 8)), -0.2, 0.2), 0.7, 1.6),
        "ref_slow": draw_ref_slow(jax.random.fold_in(splits[4], 71), 0),
    }


def centred(length):
    index = jnp.arange(length, dtype=jnp.float32)
    return jnp.where(index < length // 2, index, index - length) / length

def reference(wavefield, freqs, velocity, ref_slow):
    depth_step = 2.0
    two_pi = 2.0 * math.pi
    field = lax.complex(wavefield[0], wavefield[1])
    along_x = centred(NX)
    along_y = centred(NY)
    square = along_x[:, None] ** 2 + along_y[None, :] ** 2
    freq_col = freqs[:, None, None]
    for level in range(DEPTH):
        spectrum = jnp.fft.fft2(field, norm='ortho')
        slowness = 1.0 / velocity[level]
        lower = ref_slow[level, 0]
        upper = ref_slow[level, 1]
        upper_weight = jnp.clip((slowness - lower) / (upper - lower), 0.0, 1.0)
        weights = [1.0 - upper_weight, upper_weight]
        total = jnp.zeros_like(field)
        for branch in range(2):
            slow_ref = ref_slow[level, branch]
            target = (freq_col * slow_ref) ** 2 - square[None]
            angle = two_pi * depth_step * jnp.sqrt(jnp.abs(target))
            live = target >= 0
            shift = lax.complex(jnp.where(live, jnp.cos(angle), jnp.exp(-angle)), jnp.where(live, jnp.sin(angle), jnp.zeros_like(angle)))
            moved = jnp.fft.ifft2(spectrum * shift, norm='ortho')
            theta = two_pi * depth_step * freq_col * (slowness - slow_ref)[None]
            weight = weights[branch][None]
            total = total + weight * lax.complex(jnp.cos(theta), jnp.sin(theta)) * moved
        field = total
    return jnp.stack([jnp.real(field), jnp.imag(field)])
```

```python
import math

import jax
import jax.numpy as jnp
import numpy as np
from jax import lax
from jax.experimental import pallas as pl
from jax.experimental.pallas import tpu as pltpu
from jax.sharding import PartitionSpec as P

two_pi = 2.0 * math.pi
depth_step = 2.0

length = 2048
outer = 16
inner = 128
half = 64
rows = 64
parts = 32
sub = 8


def split_bf16(matrix):
    matrix = np.asarray(matrix, np.float32)
    high = matrix.astype(jnp.bfloat16)
    low = (matrix - high.astype(np.float32)).astype(jnp.bfloat16)
    return high, low


def dft_inner(sign):
    index = np.arange(inner)
    angle = sign * two_pi / inner * (index[:, None] * index[None, :] % inner)
    scale = 1.0 / math.sqrt(length)
    return np.cos(angle) * scale, np.sin(angle) * scale


def packed_order():
    low = np.arange(half)
    return np.concatenate([low, inner + low, half + low, inner + half + low])


def forward_y_matrix():
    real, imag = dft_inner(-1)
    full = np.block([[real, imag], [-imag, real]])
    return split_bf16(full[:, packed_order()])


def inverse_y_matrix():
    real, imag = dft_inner(1)
    full = np.block([[real, imag], [-imag, real]])
    return split_bf16(full[packed_order(), :])


def x_matrix(sign):
    real, imag = dft_inner(sign)
    return split_bf16(np.block([[real, -imag], [imag, real]]))


def y_turns():
    angle = two_pi / length * (np.arange(outer)[:, None] * np.arange(inner)[None, :])
    return np.cos(angle).astype(np.float32), np.sin(angle).astype(np.float32)


def x_turns():
    upper = (np.arange(inner) >= half).astype(np.int64)
    k = 2 * np.arange(outer // 2)[:, None, None] + upper[None, None, :]
    angle = two_pi / length * (k * np.arange(inner)[None, :, None])
    return np.cos(angle).astype(np.float32), np.sin(angle).astype(np.float32)


def lane_turns():
    upper = (np.arange(inner) >= half).astype(np.float64)
    angle = two_pi / outer * (np.arange(outer // 2)[:, None] * upper[None, :])
    return np.cos(angle).astype(np.float32), np.sin(angle).astype(np.float32)


def fit_even(function, terms):
    nodes = np.cos(np.pi * (np.arange(256) + 0.5) / 256)
    basis = np.stack([nodes ** (2 * n) for n in range(terms)], axis=1)
    solved = np.linalg.lstsq(basis, function(nodes), rcond=None)[0]
    return [float(c) for c in solved]


cos_fit = fit_even(lambda z: np.cos(np.pi * z), 9)
sin_fit = fit_even(lambda z: np.pi * np.sinc(z), 9)


def cis(cycles):
    z = 2.0 * (cycles - jnp.floor(cycles + 0.5))
    square = z * z
    cosine = cos_fit[-1]
    for c in cos_fit[-2::-1]:
        cosine = cosine * square + c
    sine = sin_fit[-1]
    for c in sin_fit[-2::-1]:
        sine = sine * square + c
    return cosine, sine * z


def times(a, b):
    return (a[0] * b[0] - a[1] * b[1], a[0] * b[1] + a[1] * b[0])


def times_conj(a, b):
    return (a[0] * b[0] + a[1] * b[1], a[1] * b[0] - a[0] * b[1])


def plus(a, b):
    return (a[0] + b[0], a[1] + b[1])


def minus(a, b):
    return (a[0] - b[0], a[1] - b[1])


def times_root(a, power, n, sign):
    eighth = (8 * power) % (8 * n)
    real, imag = a
    if eighth % n == 0:
        step = (eighth // n) % 8
        if sign < 0:
            step = (8 - step) % 8
        if step == 0:
            return a
        if step == 2:
            return (-imag, real)
        if step == 4:
            return (-real, -imag)
        if step == 6:
            return (imag, -real)
        root = math.sqrt(0.5)
        total = (real + imag) * root
        differ = (real - imag) * root
        if step == 1:
            return (differ, total)
        if step == 3:
            return (-total, differ)
        if step == 5:
            return (-differ, -total)
        return (total, -differ)
    angle = sign * two_pi * power / n
    c, s = math.cos(angle), math.sin(angle)
    return (real * c - imag * s, real * s + imag * c)


def dft(values, sign):
    n = len(values)
    if n == 2:
        return [plus(*values), minus(*values)]
    if n == 4:
        t0, t1 = plus(values[0], values[2]), minus(values[0], values[2])
        t2, t3 = plus(values[1], values[3]), minus(values[1], values[3])
        if sign > 0:
            y1 = (t1[0] - t3[1], t1[1] + t3[0])
            y3 = (t1[0] + t3[1], t1[1] - t3[0])
        else:
            y1 = (t1[0] + t3[1], t1[1] - t3[0])
            y3 = (t1[0] - t3[1], t1[1] + t3[0])
        return [plus(t0, t2), y1, minus(t0, t2), y3]
    radix = 2 if n == 8 else 4
    m = n // radix
    inside = [dft(values[s::radix], sign) for s in range(radix)]
    out = [None] * n
    for k in range(m):
        turned = [times_root(inside[s][k], s * k, n, sign) for s in range(radix)]
        for step, value in enumerate(dft(turned, sign)):
            out[k + m * step] = value
    return out


def cut(x):
    high = x.astype(jnp.bfloat16)
    low = (x - high.astype(jnp.float32)).astype(jnp.bfloat16)
    return high, low


def product(a, b):
    return jnp.dot(a, b, preferred_element_type=jnp.float32)


def mix(a, b):
    (a_high, a_low), (b_high, b_low) = a, b
    return product(a_high, b_high) + (product(a_high, b_low) + product(a_low, b_high))


def block_rows(step):
    return pl.ds(pl.multiple_of(step * sub, sub), sub)


def forward_y(read, out, spectrum, matrix_high, matrix_low, turn_cos, turn_sin):
    def step(c, carry):
        here = block_rows(c)
        values = dft([read(here, a) for a in range(outer)], -1)
        for k in range(outer):
            turn = (turn_cos[k : k + 1, :], turn_sin[k : k + 1, :])
            value = values[k] if k == 0 else times_conj(values[k], turn)
            spectrum[k, here, :inner] = value[0]
            spectrum[k, here, inner:] = value[1]
        return carry

    lax.fori_loop(0, rows // sub, step, 0)
    matrix = (matrix_high[...], matrix_low[...])
    for k in range(0, outer, 4):
        block = spectrum[k : k + 4].reshape(4 * rows, 2 * inner)
        result = mix(cut(block), matrix)
        for n in range(4):
            one = result[n * rows : (n + 1) * rows]
            out[2 * (k + n)] = one[:, :inner]
            out[2 * (k + n) + 1] = one[:, inner:]


def start_kernel(real, imag, matrix_high, matrix_low, turn_cos, turn_sin, out, spectrum):
    def read(here, a):
        columns = slice(a * inner, (a + 1) * inner)
        return real[here, columns], imag[here, columns]

    forward_y(read, out, spectrum, matrix_high, matrix_low, turn_cos, turn_sin)


def combine_kernel(
    last,
    scalars,
    moved,
    velocity,
    back_high,
    back_low,
    matrix_high,
    matrix_low,
    turn_cos,
    turn_sin,
    out,
    fields,
    weighted,
    spectrum,
):
    freq, lower, inverse_gap, turn_real, turn_imag = (scalars[n] for n in range(5))

    matrix = (back_high[...], back_low[...])
    for branch in range(2):
        for k in range(0, outer, 4):
            block = jnp.concatenate(
                [
                    jnp.concatenate([moved[2 * n, branch], moved[2 * n + 1, branch]], axis=1)
                    for n in range(k, k + 4)
                ],
                axis=0,
            )
            result = mix(cut(block), matrix)
            fields[branch, k : k + 4] = result.reshape(4, rows, 2 * inner)

    def weigh(c, carry):
        here = block_rows(c)
        for a in range(outer):
            speed = velocity[a // 2, here, (a % 2) * inner : (a % 2 + 1) * inner]
            slowness = 1.0 / speed
            excess = slowness - lower
            upper_weight = jnp.clip(excess * inverse_gap, 0.0, 1.0)
            lower_weight = 1.0 - upper_weight
            cosine, sine = cis((depth_step * freq) * excess)
            columns = slice(a * inner, (a + 1) * inner)
            weighted[0, here, columns] = lower_weight * cosine
            weighted[1, here, columns] = lower_weight * sine
            weighted[2, here, columns] = upper_weight * (cosine * turn_real - sine * turn_imag)
            weighted[3, here, columns] = upper_weight * (cosine * turn_imag + sine * turn_real)
        return carry

    lax.fori_loop(0, rows // sub, weigh, 0)

    def back(c, carry):
        here = block_rows(c)
        for branch in range(2):
            values = []
            for k in range(outer):
                value = (fields[branch, k, here, :inner], fields[branch, k, here, inner:])
                turn = (turn_cos[k : k + 1, :], turn_sin[k : k + 1, :])
                values.append(value if k == 0 else times(value, turn))
            values = dft(values, 1)
            for a in range(outer):
                columns = slice(a * inner, (a + 1) * inner)
                weight = (weighted[2 * branch, here, columns], weighted[2 * branch + 1, here, columns])
                value = times(values[a], weight)
                if last:
                    if branch == 0:
                        out[0, here, columns] = value[0]
                        out[1, here, columns] = value[1]
                    else:
                        out[0, here, columns] += value[0]
                        out[1, here, columns] += value[1]
                else:
                    if branch == 1:
                        value = (
                            value[0] + weighted[0, here, columns],
                            value[1] + weighted[1, here, columns],
                        )
                    weighted[0, here, columns] = value[0]
                    weighted[1, here, columns] = value[1]
        return carry

    lax.fori_loop(0, rows // sub, back, 0)
    if last:
        return

    def read(here, a):
        columns = slice(a * inner, (a + 1) * inner)
        return weighted[0, here, columns], weighted[1, here, columns]

    forward_y(read, out, spectrum, matrix_high, matrix_low, turn_cos, turn_sin)


def shift_kernel(
    scalars,
    square_y,
    arrived,
    there_high,
    there_low,
    back_high,
    back_low,
    turn_cos,
    turn_sin,
    lane_cos,
    lane_sin,
    out,
    spectrum,
    shifted,
):
    lane = lax.broadcasted_iota(jnp.int32, (sub, inner), 1)
    low_lanes = lane < half
    groups = outer // 2
    steps = inner // sub

    def there(c, carry):
        here = block_rows(c)
        values = []
        for a in range(groups):
            first = arrived[pl.ds(pl.multiple_of(a * inner + c * sub, sub), sub), :]
            second = arrived[pl.ds(pl.multiple_of((a + groups) * inner + c * sub, sub), sub), :]
            total, differ = first + second, first - second
            value = (
                jnp.where(low_lanes, total, pltpu.roll(differ, half, 1)),
                jnp.where(low_lanes, pltpu.roll(total, half, 1), differ),
            )
            turn = (lane_cos[a : a + 1, :], lane_sin[a : a + 1, :])
            values.append(value if a == 0 else times_conj(value, turn))
        values = dft(values, -1)
        second_half = pl.ds(pl.multiple_of(inner + c * sub, sub), sub)
        for k in range(groups):
            value = times_conj(values[k], (turn_cos[k, here, :], turn_sin[k, here, :]))
            columns = slice(k * inner, (k + 1) * inner)
            spectrum[here, columns] = value[0]
            spectrum[second_half, columns] = value[1]
        return carry

    lax.fori_loop(0, steps, there, 0)
    matrix = (there_high[...], there_low[...])
    for n in range(4):
        columns = slice(n * 2 * inner, (n + 1) * 2 * inner)
        spectrum[:, columns] = mix(matrix, cut(spectrum[:, columns]))

    sub_row = lax.broadcasted_iota(jnp.int32, (sub, inner), 0)
    fy = square_y[0:1, :]

    def propagate(c, carry):
        here = block_rows(c)
        second_half = pl.ds(pl.multiple_of(inner + c * sub, sub), sub)
        for k in range(groups):
            number = 2 * k + jnp.where(low_lanes, 0, 1) + outer * (c * sub + sub_row)
            fx = jnp.minimum(number, length - number).astype(jnp.float32) * (1.0 / length)
            square = fx * fx + fy
            columns = slice(k * inner, (k + 1) * inner)
            value = (spectrum[here, columns], spectrum[second_half, columns])
            for branch in range(2):
                target = scalars[branch] - square
                cycles = depth_step * jnp.sqrt(jnp.abs(target))
                cosine, sine = cis(cycles)
                live = target >= 0
                shift = (
                    jnp.where(live, cosine, jnp.exp(-two_pi * cycles)),
                    jnp.where(live, sine, 0.0),
                )
                moved = times(value, shift)
                shifted[branch, here, columns] = moved[0]
                shifted[branch, second_half, columns] = moved[1]
        return carry

    lax.fori_loop(0, steps, propagate, 0)
    matrix = (back_high[...], back_low[...])
    for branch in range(2):
        for n in range(4):
            columns = slice(n * 2 * inner, (n + 1) * 2 * inner)
            shifted[branch, :, columns] = mix(matrix, cut(shifted[branch, :, columns]))

    for top in range(2):

        def back(c, carry):
            position = top * half + c * sub
            here = pl.ds(pl.multiple_of(position, sub), sub)
            second_half = pl.ds(pl.multiple_of(inner + position, sub), sub)
            local = block_rows(c)
            for branch in range(2):
                values = []
                for k in range(groups):
                    columns = slice(k * inner, (k + 1) * inner)
                    value = (shifted[branch, here, columns], shifted[branch, second_half, columns])
                    values.append(times(value, (turn_cos[k, here, :], turn_sin[k, here, :])))
                values = dft(values, 1)
                for a in range(groups):
                    value = values[a]
                    if a > 0:
                        value = times(value, (lane_cos[a : a + 1, :], lane_sin[a : a + 1, :]))
                    even = jnp.where(low_lanes, value[0], pltpu.roll(value[1], half, 1))
                    odd = jnp.where(low_lanes, pltpu.roll(value[0], half, 1), value[1])
                    out[2 * a + top, branch, local, :] = even + odd
                    out[2 * (a + groups) + top, branch, local, :] = even - odd
            return carry

        lax.fori_loop(0, half // sub, back, 0)


def call(kernel, shape, scratch, operands, smem):
    vmem = pl.BlockSpec(memory_space=pltpu.VMEM)
    specs = [pl.BlockSpec(memory_space=pltpu.SMEM)] * smem + [vmem] * (len(operands) - smem)
    return pl.pallas_call(
        kernel,
        out_shape=jax.ShapeDtypeStruct(shape, jnp.float32),
        in_specs=specs,
        out_specs=vmem,
        scratch_shapes=[pltpu.VMEM(s, jnp.float32) for s in scratch],
        compiler_params=pltpu.CompilerParams(vmem_limit_bytes=28 * 1024 * 1024),
    )(*operands)


def shards(wavefield, freqs, velocity, ref_slow):
    depth = ref_slow.shape[0]
    slab_index = lax.axis_index("slab")
    freq = freqs[0]

    gathered = lax.all_gather(velocity.reshape(depth * rows, -1), "freq", axis=0, tiled=True)
    gathered = gathered.reshape(outer // 2, depth, rows, 2 * inner)

    fy_matrix = forward_y_matrix()
    iy_matrix = inverse_y_matrix()
    fx_matrix = x_matrix(-1)
    ix_matrix = x_matrix(1)
    turn_y = y_turns()
    turn_x = x_turns()
    turn_lane = lane_turns()

    lanes = jnp.arange(inner, dtype=jnp.int32) % half
    number = slab_index // 2 + outer * (half * (slab_index % 2) + lanes)
    fy = jnp.minimum(number, length - number).astype(jnp.float32) / length
    square_y = jnp.broadcast_to((fy * fy)[None, :], (sub, inner))

    packed = (parts, rows, inner)
    spectrum_shape = (outer, rows, 2 * inner)
    sent = call(
        start_kernel,
        packed,
        [spectrum_shape],
        (wavefield[0, 0], wavefield[1, 0], *fy_matrix, *turn_y),
        0,
    )
    for level in range(depth):
        lower, upper = ref_slow[level, 0], ref_slow[level, 1]
        arrived = lax.all_to_all(sent, "slab", split_axis=0, concat_axis=0, tiled=True)
        shifted = call(
            shift_kernel,
            (parts, 2, rows, inner),
            [(2 * inner, length // 2), (2, 2 * inner, length // 2)],
            (
                jnp.stack([(freq * lower) ** 2, (freq * upper) ** 2]),
                square_y,
                arrived.reshape(length, inner),
                *fx_matrix,
                *ix_matrix,
                *turn_x,
                *turn_lane,
            ),
            1,
        )
        moved = lax.all_to_all(shifted, "slab", split_axis=0, concat_axis=0, tiled=True)
        turn = two_pi * depth_step * freq * (lower - upper)
        scalars = jnp.stack([freq, lower, 1.0 / (upper - lower), jnp.cos(turn), jnp.sin(turn)])
        last = level == depth - 1

        def kernel(*refs, last=last):
            combine_kernel(last, *refs)

        sent = call(
            kernel,
            (2, rows, length) if last else packed,
            [(2, *spectrum_shape), (4, rows, length), spectrum_shape],
            (scalars, moved, gathered[:, level], *iy_matrix, *fy_matrix, *turn_y),
            1,
        )
    return sent[:, None]


def solution(mesh):
    return jax.shard_map(
        shards,
        mesh=mesh,
        in_specs=(P(None, "freq", "slab", None), P("freq"), P(None, "slab", "freq"), P()),
        out_specs=P(None, "freq", "slab", None),
        check_vma=False,
    )
```

```python
import functools
import math

import jax
import jax.numpy as jnp
import numpy as np
from jax import lax
from jax.experimental import pallas as pl
from jax.experimental.pallas import tpu as pltpu
from jax.sharding import PartitionSpec as P

two_pi = 2.0 * math.pi
depth_step = 2.0

length = 2048
outer = 16
inner = 128
half = 64
rows = 64
parts = 32
sub = 8
tile_count = 8


def split_bf16(matrix):
    matrix = np.asarray(matrix, np.float32)
    high = matrix.astype(jnp.bfloat16)
    low = (matrix - high.astype(np.float32)).astype(jnp.bfloat16)
    return high, low


def dft_inner(sign):
    index = np.arange(inner)
    angle = sign * two_pi / inner * (index[:, None] * index[None, :] % inner)
    scale = 1.0 / math.sqrt(length)
    return np.cos(angle) * scale, np.sin(angle) * scale


def packed_order():
    low = np.arange(half)
    return np.concatenate([low, inner + low, half + low, inner + half + low])


def forward_y_matrix():
    real, imag = dft_inner(-1)
    full = np.block([[real, imag], [-imag, real]])
    return split_bf16(full[:, packed_order()])


def inverse_y_matrix():
    real, imag = dft_inner(1)
    full = np.block([[real, imag], [-imag, real]])
    return split_bf16(full[packed_order(), :])


def x_matrix(sign):
    real, imag = dft_inner(sign)
    return split_bf16(np.block([[real, -imag], [imag, real]]))


def y_turns():
    angle = two_pi / length * (np.arange(outer)[:, None] * np.arange(inner)[None, :])
    return np.cos(angle).astype(np.float32), np.sin(angle).astype(np.float32)


def x_turns():
    upper = (np.arange(inner) >= half).astype(np.int64)
    k = 2 * np.arange(outer // 2)[:, None, None] + upper[None, None, :]
    angle = two_pi / length * (k * np.arange(inner)[None, :, None])
    return np.cos(angle).astype(np.float32), np.sin(angle).astype(np.float32)


def lane_turns():
    upper = (np.arange(inner) >= half).astype(np.float64)
    angle = two_pi / outer * (np.arange(outer // 2)[:, None] * upper[None, :])
    return np.cos(angle).astype(np.float32), np.sin(angle).astype(np.float32)


def fit_even(function, terms):
    nodes = np.cos(np.pi * (np.arange(256) + 0.5) / 256)
    basis = np.stack([nodes ** (2 * n) for n in range(terms)], axis=1)
    solved = np.linalg.lstsq(basis, function(nodes), rcond=None)[0]
    return [float(c) for c in solved]


cos_fit = fit_even(lambda z: np.cos(np.pi * z), 9)
sin_fit = fit_even(lambda z: np.pi * np.sinc(z), 9)


def cis(cycles):
    z = 2.0 * (cycles - jnp.floor(cycles + 0.5))
    square = z * z
    cosine = cos_fit[-1]
    for c in cos_fit[-2::-1]:
        cosine = cosine * square + c
    sine = sin_fit[-1]
    for c in sin_fit[-2::-1]:
        sine = sine * square + c
    return cosine, sine * z


def times(a, b):
    return (a[0] * b[0] - a[1] * b[1], a[0] * b[1] + a[1] * b[0])


def times_conj(a, b):
    return (a[0] * b[0] + a[1] * b[1], a[1] * b[0] - a[0] * b[1])


def plus(a, b):
    return (a[0] + b[0], a[1] + b[1])


def minus(a, b):
    return (a[0] - b[0], a[1] - b[1])


def times_root(a, power, n, sign):
    eighth = (8 * power) % (8 * n)
    real, imag = a
    if eighth % n == 0:
        step = (eighth // n) % 8
        if sign < 0:
            step = (8 - step) % 8
        if step == 0:
            return a
        if step == 2:
            return (-imag, real)
        if step == 4:
            return (-real, -imag)
        if step == 6:
            return (imag, -real)
        root = math.sqrt(0.5)
        total = (real + imag) * root
        differ = (real - imag) * root
        if step == 1:
            return (differ, total)
        if step == 3:
            return (-total, differ)
        if step == 5:
            return (-differ, -total)
        return (total, -differ)
    angle = sign * two_pi * power / n
    c, s = math.cos(angle), math.sin(angle)
    return (real * c - imag * s, real * s + imag * c)


def dft(values, sign):
    n = len(values)
    if n == 2:
        return [plus(*values), minus(*values)]
    if n == 4:
        t0, t1 = plus(values[0], values[2]), minus(values[0], values[2])
        t2, t3 = plus(values[1], values[3]), minus(values[1], values[3])
        if sign > 0:
            y1 = (t1[0] - t3[1], t1[1] + t3[0])
            y3 = (t1[0] + t3[1], t1[1] - t3[0])
        else:
            y1 = (t1[0] + t3[1], t1[1] - t3[0])
            y3 = (t1[0] - t3[1], t1[1] + t3[0])
        return [plus(t0, t2), y1, minus(t0, t2), y3]
    radix = 2 if n == 8 else 4
    m = n // radix
    inside = [dft(values[s::radix], sign) for s in range(radix)]
    out = [None] * n
    for k in range(m):
        turned = [times_root(inside[s][k], s * k, n, sign) for s in range(radix)]
        for step, value in enumerate(dft(turned, sign)):
            out[k + m * step] = value
    return out


def cut(x):
    high = x.astype(jnp.bfloat16)
    low = (x - high.astype(jnp.float32)).astype(jnp.bfloat16)
    return high, low


def product(a, b):
    return jnp.dot(a, b, preferred_element_type=jnp.float32)


def mix(a, b):
    (a_high, a_low), (b_high, b_low) = a, b
    return product(a_high, b_high) + (product(a_high, b_low) + product(a_low, b_high))


def folded(number):
    return jnp.minimum(number, length - number).astype(jnp.float32) * (1.0 / length)


def tile_of(me, n):
    group = me // 4 if n < 4 else 1 - me // 4
    return 4 * group + (me + 4 - n % 4) % 4


def block_rows(step):
    return pl.ds(pl.multiple_of(step * sub, sub), sub)


def forward_y(read, out, spectrum, matrix_high, matrix_low, turn_cos, turn_sin):
    def step(c, carry):
        here = block_rows(c)
        values = dft([read(here, a) for a in range(outer)], -1)
        for k in range(outer):
            turn = (turn_cos[k : k + 1, :], turn_sin[k : k + 1, :])
            value = values[k] if k == 0 else times_conj(values[k], turn)
            spectrum[k, here, :inner] = value[0]
            spectrum[k, here, inner:] = value[1]
        return carry

    lax.fori_loop(0, rows // sub, step, 0)
    matrix = (matrix_high[...], matrix_low[...])
    for k in range(0, outer, 4):
        block = spectrum[k : k + 4].reshape(4 * rows, 2 * inner)
        result = mix(cut(block), matrix)
        for n in range(4):
            one = result[n * rows : (n + 1) * rows]
            out[2 * (k + n)] = one[:, :inner]
            out[2 * (k + n) + 1] = one[:, inner:]


def start_kernel(
    place, freqs, ref_slow, wavefield, matrix_high, matrix_low, turn_cos, turn_sin, out, spectrum
):
    def read(here, a):
        columns = slice(a * inner, (a + 1) * inner)
        return wavefield[0, 0, here, columns], wavefield[1, 0, here, columns]

    forward_y(read, out, spectrum, matrix_high, matrix_low, turn_cos, turn_sin)


def combine_kernel(
    last,
    moved,
    weights,
    back_high,
    back_low,
    matrix_high,
    matrix_low,
    turn_cos,
    turn_sin,
    out,
    fields,
    summed,
    spectrum,
):
    matrix = (back_high[...], back_low[...])
    for branch in range(2):
        for k in range(0, outer, 4):
            block = jnp.concatenate(
                [
                    jnp.concatenate([moved[2 * n, branch], moved[2 * n + 1, branch]], axis=1)
                    for n in range(k, k + 4)
                ],
                axis=0,
            )
            result = mix(cut(block), matrix)
            fields[branch, k : k + 4] = result.reshape(4, rows, 2 * inner)

    def back(c, carry):
        here = block_rows(c)
        for branch in range(2):
            values = []
            for k in range(outer):
                value = (fields[branch, k, here, :inner], fields[branch, k, here, inner:])
                turn = (turn_cos[k : k + 1, :], turn_sin[k : k + 1, :])
                values.append(value if k == 0 else times(value, turn))
            values = dft(values, 1)
            for a in range(outer):
                columns = slice(a * inner, (a + 1) * inner)
                weight = (weights[2 * branch, a, here, :], weights[2 * branch + 1, a, here, :])
                value = times(values[a], weight)
                if branch == 1:
                    value = plus(value, (summed[0, a, here, :], summed[1, a, here, :]))
                if last and branch == 1:
                    out[0, 0, here, columns] = value[0]
                    out[1, 0, here, columns] = value[1]
                else:
                    summed[0, a, here, :] = value[0]
                    summed[1, a, here, :] = value[1]
        return carry

    lax.fori_loop(0, rows // sub, back, 0)
    if last:
        return

    def read(here, a):
        return summed[0, a, here, :], summed[1, a, here, :]

    forward_y(read, out, spectrum, matrix_high, matrix_low, turn_cos, turn_sin)


def weigh(level, place, freqs, ref_slow, tiles, weights):
    def full(value):
        return jnp.full((sub, inner), value, jnp.float32)

    lower, upper = full(ref_slow[level, 0]), full(ref_slow[level, 1])
    pace = depth_step * full(freqs[0])
    inverse_gap = 1.0 / (upper - lower)
    turn = cis(pace * (lower - upper))

    def step(c, carry):
        here = block_rows(c)
        for n in range(outer):
            slowness = 1.0 / tiles[n // 2][level, here, (n % 2) * inner : (n % 2 + 1) * inner]
            excess = slowness - lower
            upper_weight = jnp.clip(excess * inverse_gap, 0.0, 1.0)
            lower_weight = 1.0 - upper_weight
            phase = cis(pace * excess)
            other = times(phase, turn)
            a = 2 * tile_of(place[0], n // 2) + n % 2
            weights[0, a, here, :] = lower_weight * phase[0]
            weights[1, a, here, :] = lower_weight * phase[1]
            weights[2, a, here, :] = upper_weight * other[0]
            weights[3, a, here, :] = upper_weight * other[1]
        return carry

    lax.fori_loop(0, rows // sub, step, 0)


def propagators(level, place, freqs, ref_slow):
    lane = lax.broadcasted_iota(jnp.int32, (sub, inner), 1)
    sub_row = lax.broadcasted_iota(jnp.int32, (sub, inner), 0)
    fy = folded(place[1] // 2 + outer * (half * (place[1] % 2) + lane % half))
    fy = fy * fy
    squares = []
    for branch in range(2):
        wave = jnp.full((sub, inner), freqs[0]) * jnp.full((sub, inner), ref_slow[level, branch])
        squares.append(wave * wave)

    def at(c, k):
        fx = folded(2 * k + jnp.where(lane < half, 0, 1) + outer * (c * sub + sub_row))
        square = fx * fx + fy
        shifts = []
        for branch in range(2):
            target = squares[branch] - square
            cycles = depth_step * jnp.sqrt(jnp.abs(target))
            cosine, sine = cis(cycles)
            live = target >= 0
            shifts.append(
                (
                    jnp.where(live, cosine, jnp.exp(-two_pi * cycles)),
                    jnp.where(live, sine, 0.0),
                )
            )
        return shifts

    return at


def tables_kernel(depth, place, freqs, ref_slow, *refs):
    tiles, refs = refs[:tile_count], refs[tile_count:]
    for level in range(depth):
        weigh(level, place, freqs, ref_slow, tiles, refs[level])
    for level in range(1, depth):
        at = propagators(level, place, freqs, ref_slow)
        table = refs[depth + level - 1]

        def step(c, carry, at=at, table=table):
            here = block_rows(c)
            second_half = pl.ds(pl.multiple_of(inner + c * sub, sub), sub)
            for k in range(outer // 2):
                columns = slice(k * inner, (k + 1) * inner)
                for branch, shift in enumerate(at(c, k)):
                    table[branch, here, columns] = shift[0]
                    table[branch, second_half, columns] = shift[1]
            return carry

        lax.fori_loop(0, inner // sub, step, 0)


def first_shift_kernel(place, freqs, ref_slow, *refs):
    shift(propagators(0, place, freqs, ref_slow), *refs)


def later_shift_kernel(table, *refs):
    def at(c, k):
        here = block_rows(c)
        second_half = pl.ds(pl.multiple_of(inner + c * sub, sub), sub)
        columns = slice(k * inner, (k + 1) * inner)
        return [(table[n, here, columns], table[n, second_half, columns]) for n in range(2)]

    shift(at, *refs)


def shift(
    propagators_at,
    arrived,
    there_high,
    there_low,
    back_high,
    back_low,
    turn_cos,
    turn_sin,
    lane_cos,
    lane_sin,
    out,
    spectrum,
    shifted,
):
    lane = lax.broadcasted_iota(jnp.int32, (sub, inner), 1)
    low_lanes = lane < half
    groups = outer // 2
    steps = inner // sub

    def there(c, carry):
        here = block_rows(c)
        values = []
        for a in range(groups):
            first = arrived[pl.ds(pl.multiple_of(a * inner + c * sub, sub), sub), :]
            second = arrived[pl.ds(pl.multiple_of((a + groups) * inner + c * sub, sub), sub), :]
            total, differ = first + second, first - second
            value = (
                jnp.where(low_lanes, total, pltpu.roll(differ, half, 1)),
                jnp.where(low_lanes, pltpu.roll(total, half, 1), differ),
            )
            turn = (lane_cos[a : a + 1, :], lane_sin[a : a + 1, :])
            values.append(value if a == 0 else times_conj(value, turn))
        values = dft(values, -1)
        second_half = pl.ds(pl.multiple_of(inner + c * sub, sub), sub)
        for k in range(groups):
            value = times_conj(values[k], (turn_cos[k, here, :], turn_sin[k, here, :]))
            columns = slice(k * inner, (k + 1) * inner)
            spectrum[here, columns] = value[0]
            spectrum[second_half, columns] = value[1]
        return carry

    lax.fori_loop(0, steps, there, 0)
    matrix = (there_high[...], there_low[...])
    for n in range(4):
        columns = slice(n * 2 * inner, (n + 1) * 2 * inner)
        spectrum[:, columns] = mix(matrix, cut(spectrum[:, columns]))

    def propagate(c, carry):
        here = block_rows(c)
        second_half = pl.ds(pl.multiple_of(inner + c * sub, sub), sub)
        for k in range(groups):
            columns = slice(k * inner, (k + 1) * inner)
            value = (spectrum[here, columns], spectrum[second_half, columns])
            for branch, factor in enumerate(propagators_at(c, k)):
                moved = times(value, factor)
                shifted[branch, here, columns] = moved[0]
                shifted[branch, second_half, columns] = moved[1]
        return carry

    lax.fori_loop(0, steps, propagate, 0)
    matrix = (back_high[...], back_low[...])
    for branch in range(2):
        for n in range(4):
            columns = slice(n * 2 * inner, (n + 1) * 2 * inner)
            shifted[branch, :, columns] = mix(matrix, cut(shifted[branch, :, columns]))

    for top in range(2):

        def back(c, carry):
            position = top * half + c * sub
            here = pl.ds(pl.multiple_of(position, sub), sub)
            second_half = pl.ds(pl.multiple_of(inner + position, sub), sub)
            local = block_rows(c)
            for branch in range(2):
                values = []
                for k in range(groups):
                    columns = slice(k * inner, (k + 1) * inner)
                    value = (shifted[branch, here, columns], shifted[branch, second_half, columns])
                    values.append(times(value, (turn_cos[k, here, :], turn_sin[k, here, :])))
                values = dft(values, 1)
                for a in range(groups):
                    value = values[a]
                    if a > 0:
                        value = times(value, (lane_cos[a : a + 1, :], lane_sin[a : a + 1, :]))
                    even = jnp.where(low_lanes, value[0], pltpu.roll(value[1], half, 1))
                    odd = jnp.where(low_lanes, pltpu.roll(value[0], half, 1), value[1])
                    out[2 * a + top, branch, local, :] = even + odd
                    out[2 * (a + groups) + top, branch, local, :] = even - odd
            return carry

        lax.fori_loop(0, half // sub, back, 0)


def call(kernel, shapes, scratch, scalars, operands):
    vmem = pl.BlockSpec(memory_space=pltpu.VMEM)
    smem = pl.BlockSpec(memory_space=pltpu.SMEM)
    return pl.pallas_call(
        kernel,
        out_shape=[jax.ShapeDtypeStruct(s, jnp.float32) for s in shapes],
        in_specs=[smem] * len(scalars) + [vmem] * len(operands),
        out_specs=[vmem] * len(shapes),
        scratch_shapes=[pltpu.VMEM(s, jnp.float32) for s in scratch],
        compiler_params=pltpu.CompilerParams(vmem_limit_bytes=28 * 1024 * 1024),
    )(*scalars, *operands)


def velocity_tiles(velocity):
    other = lax.ppermute(velocity, "freq", [(n, (n + 4) % 8) for n in range(8)])
    tiles = []
    for tile in (velocity, other):
        tiles.append(tile)
        for back in range(1, 4):
            pairs = [(n, n // 4 * 4 + (n + back) % 4) for n in range(8)]
            tiles.append(lax.ppermute(tile, "freq", pairs))
    return tiles


def exchange(values):
    return lax.all_to_all(values, "slab", split_axis=0, concat_axis=0, tiled=True)


def shards(wavefield, freqs, velocity, ref_slow):
    depth = ref_slow.shape[0]
    place = jnp.stack([lax.axis_index("freq"), lax.axis_index("slab")])
    common = (place, freqs, ref_slow)
    tiles = velocity_tiles(velocity)

    fy_matrix = forward_y_matrix()
    iy_matrix = inverse_y_matrix()
    fx_matrix = x_matrix(-1)
    ix_matrix = x_matrix(1)
    turn_y = y_turns()
    turn_x = x_turns()
    turn_lane = lane_turns()

    packed = (parts, rows, inner)
    spectrum_shape = (outer, rows, 2 * inner)
    folded_shape = (2 * inner, length // 2)
    weights_shape = (4, outer, rows, inner)
    (sent,) = call(
        start_kernel, [packed], [spectrum_shape], common, (wavefield, *fy_matrix, *turn_y)
    )
    tables = call(
        functools.partial(tables_kernel, depth),
        [weights_shape] * depth + [(2, *folded_shape)] * (depth - 1),
        [],
        common,
        velocity_tiles(velocity),
    )
    for level in range(depth):
        arrived = exchange(sent).reshape(length, inner)
        (shifted,) = call(
            later_shift_kernel if level else first_shift_kernel,
            [(parts, 2, rows, inner)],
            [folded_shape, (2, *folded_shape)],
            () if level else common,
            (
                *tables[depth + level - 1 : depth + level][: 1 if level else 0],
                arrived,
                *fx_matrix,
                *ix_matrix,
                *turn_x,
                *turn_lane,
            ),
        )
        moved = exchange(shifted)
        last = level == depth - 1
        (sent,) = call(
            functools.partial(combine_kernel, last),
            [(2, 1, rows, length) if last else packed],
            [(2, *spectrum_shape), (2, outer, rows, inner), spectrum_shape],
            (),
            (moved, tables[level], *iy_matrix, *fy_matrix, *turn_y),
        )
    return sent


def solution(mesh):
    return jax.shard_map(
        shards,
        mesh=mesh,
        in_specs=(P(None, "freq", "slab", None), P("freq"), P(None, "slab", "freq"), P()),
        out_specs=P(None, "freq", "slab", None),
        check_vma=False,
    )
```

```python
import functools
import math

import jax
import jax.numpy as jnp
import numpy as np
from jax import lax
from jax.experimental import pallas as pl
from jax.experimental.pallas import tpu as pltpu
from jax.sharding import Mesh
from jax.sharding import PartitionSpec as P

two_pi = 2.0 * math.pi
depth_step = 2.0

length = 2048
outer = 16
inner = 128
half = 64
rows = 64
parts = 32
sub = 8
depth = 3
ring = 8
quarter = 16
cell_start = 8 * rows
freq_start = cell_start + depth * 2 * quarter
message = freq_start + sub


def split_bf16(matrix):
    matrix = np.asarray(matrix, np.float32)
    high = matrix.astype(jnp.bfloat16)
    low = (matrix - high.astype(np.float32)).astype(jnp.bfloat16)
    return high, low


def dft_inner(sign):
    index = np.arange(inner)
    angle = sign * two_pi / inner * (index[:, None] * index[None, :] % inner)
    scale = 1.0 / math.sqrt(length)
    return np.cos(angle) * scale, np.sin(angle) * scale


def packed_order():
    low = np.arange(half)
    return np.concatenate([low, inner + low, half + low, inner + half + low])


def forward_y_matrix():
    real, imag = dft_inner(-1)
    full = np.block([[real, imag], [-imag, real]])
    return split_bf16(full[:, packed_order()])


def inverse_y_matrix():
    real, imag = dft_inner(1)
    full = np.block([[real, imag], [-imag, real]])
    return split_bf16(full[packed_order(), :])


def x_matrix(sign):
    real, imag = dft_inner(sign)
    return split_bf16(np.block([[real, -imag], [imag, real]]))


def y_turns():
    angle = two_pi / length * (np.arange(outer)[:, None] * np.arange(inner)[None, :])
    return np.cos(angle).astype(np.float32), np.sin(angle).astype(np.float32)


def x_turns():
    upper = (np.arange(inner) >= half).astype(np.int64)
    k = 2 * np.arange(outer // 2)[:, None, None] + upper[None, None, :]
    angle = two_pi / length * (k * np.arange(inner)[None, :, None])
    return np.cos(angle).astype(np.float32), np.sin(angle).astype(np.float32)


def lane_turns():
    upper = (np.arange(inner) >= half).astype(np.float64)
    angle = two_pi / outer * (np.arange(outer // 2)[:, None] * upper[None, :])
    return np.cos(angle).astype(np.float32), np.sin(angle).astype(np.float32)


def fit_even(function, terms):
    nodes = np.cos(np.pi * (np.arange(256) + 0.5) / 256)
    basis = np.stack([nodes ** (2 * n) for n in range(terms)], axis=1)
    solved = np.linalg.lstsq(basis, function(nodes), rcond=None)[0]
    return [float(c) for c in solved]


cos_fit = fit_even(lambda z: np.cos(np.pi * z), 9)
sin_fit = fit_even(lambda z: np.pi * np.sinc(z), 9)


def cis(cycles):
    z = 2.0 * (cycles - jnp.floor(cycles + 0.5))
    square = z * z
    cosine = cos_fit[-1]
    for c in cos_fit[-2::-1]:
        cosine = cosine * square + c
    sine = sin_fit[-1]
    for c in sin_fit[-2::-1]:
        sine = sine * square + c
    return cosine, sine * z


def times(a, b):
    return (a[0] * b[0] - a[1] * b[1], a[0] * b[1] + a[1] * b[0])


def times_conj(a, b):
    return (a[0] * b[0] + a[1] * b[1], a[1] * b[0] - a[0] * b[1])


def plus(a, b):
    return (a[0] + b[0], a[1] + b[1])


def minus(a, b):
    return (a[0] - b[0], a[1] - b[1])


def times_root(a, power, n, sign):
    eighth = (8 * power) % (8 * n)
    real, imag = a
    if eighth % n == 0:
        step = (eighth // n) % 8
        if sign < 0:
            step = (8 - step) % 8
        if step == 0:
            return a
        if step == 2:
            return (-imag, real)
        if step == 4:
            return (-real, -imag)
        if step == 6:
            return (imag, -real)
        root = math.sqrt(0.5)
        total = (real + imag) * root
        differ = (real - imag) * root
        if step == 1:
            return (differ, total)
        if step == 3:
            return (-total, differ)
        if step == 5:
            return (-differ, -total)
        return (total, -differ)
    angle = sign * two_pi * power / n
    c, s = math.cos(angle), math.sin(angle)
    return (real * c - imag * s, real * s + imag * c)


def dft(values, sign):
    n = len(values)
    if n == 2:
        return [plus(*values), minus(*values)]
    if n == 4:
        t0, t1 = plus(values[0], values[2]), minus(values[0], values[2])
        t2, t3 = plus(values[1], values[3]), minus(values[1], values[3])
        if sign > 0:
            y1 = (t1[0] - t3[1], t1[1] + t3[0])
            y3 = (t1[0] + t3[1], t1[1] - t3[0])
        else:
            y1 = (t1[0] + t3[1], t1[1] - t3[0])
            y3 = (t1[0] - t3[1], t1[1] + t3[0])
        return [plus(t0, t2), y1, minus(t0, t2), y3]
    radix = 2 if n == 8 else 4
    m = n // radix
    inside = [dft(values[s::radix], sign) for s in range(radix)]
    out = [None] * n
    for k in range(m):
        turned = [times_root(inside[s][k], s * k, n, sign) for s in range(radix)]
        for step, value in enumerate(dft(turned, sign)):
            out[k + m * step] = value
    return out


def cut(x):
    high = x.astype(jnp.bfloat16)
    low = (x - high.astype(jnp.float32)).astype(jnp.bfloat16)
    return high, low


def product(a, b):
    return jnp.dot(a, b, preferred_element_type=jnp.float32)


def mix(a, b):
    (a_high, a_low), (b_high, b_low) = a, b
    return product(a_high, b_high) + (product(a_high, b_low) + product(a_low, b_high))


def folded(number):
    return jnp.minimum(number, length - number).astype(jnp.float32) * (1.0 / length)


def block_rows(step):
    return pl.ds(pl.multiple_of(step * sub, sub), sub)


def forward_y(read, write, spectrum, matrices, turns):
    turn_cos, turn_sin = turns[0], turns[1]

    def step(c, carry):
        here = block_rows(c)
        values = dft([read(here, a) for a in range(outer)], -1)
        for k in range(outer):
            turn = (turn_cos[k : k + 1, :], turn_sin[k : k + 1, :])
            value = values[k] if k == 0 else times_conj(values[k], turn)
            spectrum[k, here, :inner] = value[0]
            spectrum[k, here, inner:] = value[1]
        return carry

    lax.fori_loop(0, rows // sub, step, 0)
    matrix = (matrices[0], matrices[1])
    for k in range(0, outer, 4):
        block = spectrum[k : k + 4].reshape(4 * rows, 2 * inner)
        result = mix(cut(block), matrix)
        for n in range(4):
            one = result[n * rows : (n + 1) * rows]
            write(2 * (k + n), one[:, :inner])
            write(2 * (k + n) + 1, one[:, inner:])


def start_kernel(freqs, wavefield, velocity, matrices, turns, out, spectrum):
    def read(here, a):
        columns = slice(a * inner, (a + 1) * inner)
        return wavefield[0, 0, here, columns], wavefield[1, 0, here, columns]

    def write(part, value):
        y, x, c = part // 8, part // 2 % 4, part % 2
        place = (4 * c + x) * rows
        out[y, place : place + rows, :] = value

    forward_y(read, write, spectrum, matrices, turns)
    for y in range(4):
        for level in range(depth):
            for t in range(2):
                place = cell_start + (2 * level + t) * quarter
                out[y, place : place + quarter, :] = velocity[
                    level, y * quarter : (y + 1) * quarter, t * inner : (t + 1) * inner
                ]
        out[y, freq_start:, :] = jnp.full((sub, inner), freqs[0], jnp.float32)


def combine_kernel(
    last,
    moved,
    weights,
    back_matrices,
    matrices,
    turns,
    out,
    fields,
    summed,
    spectrum,
):
    turn_cos, turn_sin = turns[0], turns[1]
    matrix = (back_matrices[0], back_matrices[1])
    for branch in range(2):
        for k in range(0, outer, 4):
            block = jnp.concatenate(
                [
                    jnp.concatenate([moved[2 * n, branch], moved[2 * n + 1, branch]], axis=1)
                    for n in range(k, k + 4)
                ],
                axis=0,
            )
            result = mix(cut(block), matrix)
            fields[branch, k : k + 4] = result.reshape(4, rows, 2 * inner)

    def back(c, carry):
        here = block_rows(c)
        for branch in range(2):
            values = []
            for k in range(outer):
                value = (fields[branch, k, here, :inner], fields[branch, k, here, inner:])
                turn = (turn_cos[k : k + 1, :], turn_sin[k : k + 1, :])
                values.append(value if k == 0 else times(value, turn))
            values = dft(values, 1)
            for a in range(outer):
                weight = (weights[2 * branch, a, here, :], weights[2 * branch + 1, a, here, :])
                value = times(values[a], weight)
                if branch == 1:
                    value = plus(value, (summed[0, a, here, :], summed[1, a, here, :]))
                if last and branch == 1:
                    columns = slice(a * inner, (a + 1) * inner)
                    inside = pl.ds(pl.multiple_of(c % 2 * sub, sub), sub)
                    out[c // 2, 0, inside, columns] = value[0]
                    out[c // 2, 1, inside, columns] = value[1]
                else:
                    summed[0, a, here, :] = value[0]
                    summed[1, a, here, :] = value[1]
        return carry

    lax.fori_loop(0, rows // sub, back, 0)
    if last:
        return

    def read(here, a):
        return summed[0, a, here, :], summed[1, a, here, :]

    def write(part, value):
        out[part] = value

    forward_y(read, write, spectrum, matrices, turns)


def weigh_kernel(level, place, freqs, ref_slow, *refs):
    def full(value):
        return jnp.full((sub, inner), value, jnp.float32)

    lower, upper = full(ref_slow[level, 0]), full(ref_slow[level, 1])
    pace = depth_step * full(freqs[place[0]])
    inverse_gap = 1.0 / (upper - lower)
    turn = cis(pace * (lower - upper))

    tiles, weights = refs[:ring], refs[ring]
    z = 2 * place[0] + place[1]
    for n in range(ring):
        source = (z + n) % ring
        tile = tiles[n]

        def step(c, carry, source=source, tile=tile):
            from_y = c // 2
            inside = pl.ds(pl.multiple_of(c % 2 * sub, sub), sub)
            here = pl.ds(pl.multiple_of(source // 2 * quarter + c % 2 * sub, sub), sub)
            for t in range(2):
                slowness = 1.0 / tile[from_y, 2 * level + t, inside, :]
                excess = slowness - lower
                upper_weight = jnp.clip(excess * inverse_gap, 0.0, 1.0)
                lower_weight = 1.0 - upper_weight
                phase = cis(pace * excess)
                other = times(phase, turn)
                a = 2 * (source % 2 * 4 + from_y) + t
                weights[0, a, here, :] = lower_weight * phase[0]
                weights[1, a, here, :] = lower_weight * phase[1]
                weights[2, a, here, :] = upper_weight * other[0]
                weights[3, a, here, :] = upper_weight * other[1]
            return carry

        lax.fori_loop(0, 8, step, 0, unroll=2)


def propagators(level, place, freqs, ref_slow):
    lane = lax.broadcasted_iota(jnp.int32, (sub, inner), 1)
    sub_row = lax.broadcasted_iota(jnp.int32, (sub, inner), 0)
    fy = folded(place[2] // 2 + outer * (half * (place[2] % 2) + lane % half))
    fy = fy * fy
    squares = []
    for branch in range(2):
        wave = jnp.full((sub, inner), freqs[place[0]]) * jnp.full((sub, inner), ref_slow[level, branch])
        squares.append(wave * wave)

    def at(c, k):
        fx = folded(2 * k + jnp.where(lane < half, 0, 1) + outer * (c * sub + sub_row))
        square = fx * fx + fy
        shifts = []
        for branch in range(2):
            target = squares[branch] - square
            cycles = depth_step * jnp.sqrt(jnp.abs(target))
            cosine, sine = cis(cycles)
            live = target >= 0
            shifts.append(
                (
                    jnp.where(live, cosine, jnp.exp(-two_pi * cycles)),
                    jnp.where(live, sine, 0.0),
                )
            )
        return shifts

    return at


def propagator_kernel(level, place, freqs, ref_slow, table):
    at = propagators(level, place, freqs, ref_slow)

    def step(c, carry):
        here = block_rows(c)
        second_half = pl.ds(pl.multiple_of(inner + c * sub, sub), sub)
        for k in range(outer // 2):
            columns = slice(k * inner, (k + 1) * inner)
            for branch, factor in enumerate(at(c, k)):
                table[branch, here, columns] = factor[0]
                table[branch, second_half, columns] = factor[1]
        return carry

    lax.fori_loop(0, inner // sub, step, 0)


def slab_rows(a, top, c):
    return ((a // 4 * 2 + top) * 4 + a % 4) * rows + c * sub


def plane_chunk(a, top, c):
    return c // 2 * 8 + a % 4 * 2 + top, a // 4 * quarter + c % 2 * sub


def plane_rows(a, top, c):
    chunk, row = plane_chunk(a, top, c)
    return chunk * rows + row


def shift_kernel(
    rows_of,
    arrived,
    table,
    there_matrices,
    back_matrices,
    turns,
    lane_turn,
    out,
    spectrum,
    shifted,
):
    lane = lax.broadcasted_iota(jnp.int32, (sub, inner), 1)
    low_lanes = lane < half
    groups = outer // 2
    steps = inner // sub

    def there(top, c, carry):
        position = top * half + c * sub
        here = pl.ds(pl.multiple_of(position, sub), sub)
        second_half = pl.ds(pl.multiple_of(inner + position, sub), sub)
        values = []
        for a in range(groups):
            first = arrived[pl.ds(pl.multiple_of(rows_of(a, top, c), sub), sub), :]
            second = arrived[pl.ds(pl.multiple_of(rows_of(a + groups, top, c), sub), sub), :]
            total, differ = first + second, first - second
            value = (
                jnp.where(low_lanes, total, pltpu.roll(differ, half, 1)),
                jnp.where(low_lanes, pltpu.roll(total, half, 1), differ),
            )
            turn = (lane_turn[0, a : a + 1, :], lane_turn[1, a : a + 1, :])
            values.append(value if a == 0 else times_conj(value, turn))
        values = dft(values, -1)
        for k in range(groups):
            value = times_conj(values[k], (turns[0, k, here, :], turns[1, k, here, :]))
            columns = slice(k * inner, (k + 1) * inner)
            spectrum[here, columns] = value[0]
            spectrum[second_half, columns] = value[1]
        return carry

    for top in range(2):
        lax.fori_loop(0, half // sub, functools.partial(there, top), 0)
    matrix = (there_matrices[0], there_matrices[1])
    for n in range(4):
        columns = slice(n * 2 * inner, (n + 1) * 2 * inner)
        spectrum[:, columns] = mix(matrix, cut(spectrum[:, columns]))

    def propagate(c, carry):
        here = block_rows(c)
        second_half = pl.ds(pl.multiple_of(inner + c * sub, sub), sub)
        for k in range(groups):
            columns = slice(k * inner, (k + 1) * inner)
            value = (spectrum[here, columns], spectrum[second_half, columns])
            for branch in range(2):
                moved = times(value, (table[branch, here, columns], table[branch, second_half, columns]))
                shifted[branch, here, columns] = moved[0]
                shifted[branch, second_half, columns] = moved[1]
        return carry

    lax.fori_loop(0, steps, propagate, 0)
    matrix = (back_matrices[0], back_matrices[1])
    for branch in range(2):
        for n in range(4):
            columns = slice(n * 2 * inner, (n + 1) * 2 * inner)
            shifted[branch, :, columns] = mix(matrix, cut(shifted[branch, :, columns]))

    for top in range(2):

        def back(c, carry, top=top):
            position = top * half + c * sub
            here = pl.ds(pl.multiple_of(position, sub), sub)
            second_half = pl.ds(pl.multiple_of(inner + position, sub), sub)
            for branch in range(2):
                values = []
                for k in range(groups):
                    columns = slice(k * inner, (k + 1) * inner)
                    value = (shifted[branch, here, columns], shifted[branch, second_half, columns])
                    values.append(times(value, (turns[0, k, here, :], turns[1, k, here, :])))
                values = dft(values, 1)
                for a in range(groups):
                    value = values[a]
                    if a > 0:
                        value = times(value, (lane_turn[0, a : a + 1, :], lane_turn[1, a : a + 1, :]))
                    even = jnp.where(low_lanes, value[0], pltpu.roll(value[1], half, 1))
                    odd = jnp.where(low_lanes, pltpu.roll(value[0], half, 1), value[1])
                    for at, result in ((a, even + odd), (a + groups, even - odd)):
                        chunk, row = plane_chunk(at, top, c)
                        out[chunk, branch, pl.ds(pl.multiple_of(row, sub), sub), :] = result
            return carry

        lax.fori_loop(0, half // sub, back, 0)


def call(kernel, shapes, scratch, scalars, operands):
    vmem = pl.BlockSpec(memory_space=pltpu.VMEM)
    smem = pl.BlockSpec(memory_space=pltpu.SMEM)
    return pl.pallas_call(
        kernel,
        out_shape=[jax.ShapeDtypeStruct(s, jnp.float32) for s in shapes],
        in_specs=[smem] * len(scalars) + [vmem] * len(operands),
        out_specs=[vmem] * len(shapes),
        scratch_shapes=[pltpu.VMEM(s, jnp.float32) for s in scratch],
        compiler_params=pltpu.CompilerParams(vmem_limit_bytes=28 * 1024 * 1024),
    )(*scalars, *operands)


def exchange(values, axes):
    return lax.all_to_all(values, axes, split_axis=0, concat_axis=0, tiled=True)


def around_z(tile):
    axes = ("zl", "zh")
    index = [n % 2 * 4 + n // 2 for n in range(ring)]
    down = [(index[n], index[n - 1]) for n in range(ring)]
    up = [(index[n - 1], index[n]) for n in range(ring)]
    tiles = [tile] + [None] * (ring - 1)
    above = below = tile
    for n in range(1, 5):
        above = lax.ppermute(above, axes, down)
        tiles[n] = above
        if n < 4:
            below = lax.ppermute(below, axes, up)
            tiles[ring - n] = below
    return tiles


def shards(wavefield, freqs, velocity, ref_slow):
    zh, zl = lax.axis_index("zh"), lax.axis_index("zl")
    part = (lax.axis_index("y") * 4 + lax.axis_index("x")) * 2 + lax.axis_index("c")
    place = jnp.stack([zh, zl, part])

    fy_matrix = np.stack(forward_y_matrix())
    iy_matrix = np.stack(inverse_y_matrix())
    fx_matrix = np.stack(x_matrix(-1))
    ix_matrix = np.stack(x_matrix(1))
    turn_y = np.stack(y_turns())
    turn_x = np.stack(x_turns())
    turn_lane = np.stack(lane_turns())

    plane = ("y", "x", "c")
    packed = (parts, rows, inner)
    spectrum_shape = (outer, rows, 2 * inner)
    folded_shape = (2 * inner, length // 2)
    (sent,) = call(
        start_kernel,
        [(4, message, inner)],
        [spectrum_shape],
        (freqs,),
        (wavefield, velocity, fy_matrix, turn_y),
    )
    sent = exchange(sent, ("y",))
    freqs = sent[:, freq_start, 0]
    tile = sent[:, cell_start:freq_start].reshape(4, 2 * depth, quarter, inner)
    arrived = exchange(sent[:, :cell_start].reshape(packed), ("zh", "c", "x"))
    arrived, tile = lax.optimization_barrier((arrived, tile))
    tiles = around_z(tile)
    common = (place, freqs, ref_slow)
    for level in range(depth):
        if level:
            arrived = exchange(sent, plane)
        (table,) = call(
            functools.partial(propagator_kernel, level), [(2, *folded_shape)], [], common, ()
        )
        (shifted,) = call(
            functools.partial(shift_kernel, plane_rows if level else slab_rows),
            [(parts, 2, rows, inner)],
            [folded_shape, (2, *folded_shape)],
            (),
            (arrived.reshape(length, inner), table, fx_matrix, ix_matrix, turn_x, turn_lane),
        )
        moved = exchange(shifted, plane)
        (weights,) = call(
            functools.partial(weigh_kernel, level), [(4, outer, rows, inner)], [], common, tiles
        )
        last = level == depth - 1
        (sent,) = call(
            functools.partial(combine_kernel, last),
            [(4, 2, quarter, length) if last else packed],
            [(2, *spectrum_shape), (2, outer, rows, inner), spectrum_shape],
            (),
            (moved, weights, iy_matrix, fy_matrix, turn_y),
        )
    back = exchange(exchange(sent, ("zh",)), ("y",))
    return back.transpose(1, 0, 2, 3).reshape(2, 1, rows, length)


def solution(mesh):
    axes = ("zl", "y", "zh", "x", "c")
    return jax.shard_map(
        shards,
        mesh=Mesh(mesh.devices.reshape(2, 4, 4, 4, 2), axes),
        in_specs=(
            P(None, axes[:2], axes[2:], None),
            P(axes[:2]),
            P(None, axes[2:], axes[:2]),
            P(),
        ),
        out_specs=P(None, axes[:2], axes[2:], None),
        check_vma=False,
    )
```

```python
import functools
import math

import jax
import jax.numpy as jnp
import numpy as np
from jax import lax
from jax.experimental import pallas as pl
from jax.experimental.pallas import tpu as pltpu
from jax.sharding import Mesh
from jax.sharding import PartitionSpec as P

two_pi = 2.0 * math.pi
depth_step = 2.0

length = 2048
outer = 16
inner = 128
half = 64
rows = 64
parts = 32
sub = 8
depth = 3
ring = 8
quarter = 16
freq_start = depth * 2 * quarter
message = freq_start + sub


def split_bf16(matrix):
    matrix = np.asarray(matrix, np.float32)
    high = matrix.astype(jnp.bfloat16)
    low = (matrix - high.astype(np.float32)).astype(jnp.bfloat16)
    return high, low


def dft_inner(sign):
    index = np.arange(inner)
    angle = sign * two_pi / inner * (index[:, None] * index[None, :] % inner)
    scale = 1.0 / math.sqrt(length)
    return np.cos(angle) * scale, np.sin(angle) * scale


def packed_order():
    low = np.arange(half)
    return np.concatenate([low, inner + low, half + low, inner + half + low])


def forward_y_matrix():
    real, imag = dft_inner(-1)
    full = np.block([[real, imag], [-imag, real]])
    return split_bf16(full[:, packed_order()])


def inverse_y_matrix():
    real, imag = dft_inner(1)
    full = np.block([[real, imag], [-imag, real]])
    return split_bf16(full[packed_order(), :])


def x_matrix(sign):
    real, imag = dft_inner(sign)
    return split_bf16(np.block([[real, -imag], [imag, real]]))


def x_turns():
    upper = (np.arange(inner) >= half).astype(np.int64)
    k = 2 * np.arange(outer // 2)[:, None, None] + upper[None, None, :]
    angle = two_pi / length * (k * np.arange(inner)[None, :, None])
    return np.cos(angle).astype(np.float32), np.sin(angle).astype(np.float32)


def fit_even(function, terms):
    nodes = np.cos(np.pi * (np.arange(256) + 0.5) / 256)
    basis = np.stack([nodes ** (2 * n) for n in range(terms)], axis=1)
    solved = np.linalg.lstsq(basis, function(nodes), rcond=None)[0]
    return [float(c) for c in solved]


cos_fit = fit_even(lambda z: np.cos(np.pi * z), 9)
sin_fit = fit_even(lambda z: np.pi * np.sinc(z), 9)


def cis(cycles):
    z = 2.0 * (cycles - jnp.floor(cycles + 0.5))
    square = z * z
    cosine = cos_fit[-1]
    for c in cos_fit[-2::-1]:
        cosine = cosine * square + c
    sine = sin_fit[-1]
    for c in sin_fit[-2::-1]:
        sine = sine * square + c
    return cosine, sine * z


def fill_y_turns(turns):
    k = lax.broadcasted_iota(jnp.int32, (outer, inner), 0)
    b = lax.broadcasted_iota(jnp.int32, (outer, inner), 1)
    turns[0], turns[1] = cis((k * b).astype(jnp.float32) * (1.0 / length))


def fill_lane_turns(turns):
    a = lax.broadcasted_iota(jnp.int32, (outer // 2, inner), 0)
    lane = lax.broadcasted_iota(jnp.int32, (outer // 2, inner), 1)
    turns[0], turns[1] = cis(jnp.where(lane < half, 0, a).astype(jnp.float32) * (1.0 / outer))


def times(a, b):
    return (a[0] * b[0] - a[1] * b[1], a[0] * b[1] + a[1] * b[0])


def times_conj(a, b):
    return (a[0] * b[0] + a[1] * b[1], a[1] * b[0] - a[0] * b[1])


def plus(a, b):
    return (a[0] + b[0], a[1] + b[1])


def minus(a, b):
    return (a[0] - b[0], a[1] - b[1])


def times_root(a, power, n, sign):
    eighth = (8 * power) % (8 * n)
    real, imag = a
    if eighth % n == 0:
        step = (eighth // n) % 8
        if sign < 0:
            step = (8 - step) % 8
        if step == 0:
            return a
        if step == 2:
            return (-imag, real)
        if step == 4:
            return (-real, -imag)
        if step == 6:
            return (imag, -real)
        root = math.sqrt(0.5)
        total = (real + imag) * root
        differ = (real - imag) * root
        if step == 1:
            return (differ, total)
        if step == 3:
            return (-total, differ)
        if step == 5:
            return (-differ, -total)
        return (total, -differ)
    angle = sign * two_pi * power / n
    c, s = math.cos(angle), math.sin(angle)
    return (real * c - imag * s, real * s + imag * c)


def dft(values, sign):
    n = len(values)
    if n == 2:
        return [plus(*values), minus(*values)]
    if n == 4:
        t0, t1 = plus(values[0], values[2]), minus(values[0], values[2])
        t2, t3 = plus(values[1], values[3]), minus(values[1], values[3])
        if sign > 0:
            y1 = (t1[0] - t3[1], t1[1] + t3[0])
            y3 = (t1[0] + t3[1], t1[1] - t3[0])
        else:
            y1 = (t1[0] + t3[1], t1[1] - t3[0])
            y3 = (t1[0] - t3[1], t1[1] + t3[0])
        return [plus(t0, t2), y1, minus(t0, t2), y3]
    radix = 2 if n == 8 else 4
    m = n // radix
    inside = [dft(values[s::radix], sign) for s in range(radix)]
    out = [None] * n
    for k in range(m):
        turned = [times_root(inside[s][k], s * k, n, sign) for s in range(radix)]
        for step, value in enumerate(dft(turned, sign)):
            out[k + m * step] = value
    return out


def cut(x):
    high = x.astype(jnp.bfloat16)
    low = (x - high.astype(jnp.float32)).astype(jnp.bfloat16)
    return high, low


def product(a, b):
    return jnp.dot(a, b, preferred_element_type=jnp.float32)


def mix(a, b):
    (a_high, a_low), (b_high, b_low) = a, b
    return product(a_high, b_high) + (product(a_high, b_low) + product(a_low, b_high))


def folded(number):
    return jnp.minimum(number, length - number).astype(jnp.float32) * (1.0 / length)


def block_rows(step):
    return pl.ds(pl.multiple_of(step * sub, sub), sub)


def forward_y(read, write, spectrum, matrices, turns):
    turn_cos, turn_sin = turns[0], turns[1]

    def step(c, carry):
        here = block_rows(c)
        values = dft([read(here, a) for a in range(outer)], -1)
        for k in range(outer):
            turn = (turn_cos[k : k + 1, :], turn_sin[k : k + 1, :])
            value = values[k] if k == 0 else times_conj(values[k], turn)
            spectrum[k, here, :inner] = value[0]
            spectrum[k, here, inner:] = value[1]
        return carry

    lax.fori_loop(0, rows // sub, step, 0)
    matrix = (matrices[0], matrices[1])
    for k in range(0, outer, 4):
        block = spectrum[k : k + 4].reshape(4 * rows, 2 * inner)
        result = mix(cut(block), matrix)
        for n in range(4):
            one = result[n * rows : (n + 1) * rows]
            write(2 * (k + n), one[:, :inner])
            write(2 * (k + n) + 1, one[:, inner:])


def carve_kernel(place, freqs, velocity, *pieces):
    for n, piece in enumerate(pieces):
        first = (place[3] + n) % 4 * quarter
        for level in range(depth):
            for t in range(2):
                at = (2 * level + t) * quarter
                here = pl.ds(pl.multiple_of(first, quarter), quarter)
                piece[at : at + quarter, :] = velocity[level, here, t * inner : (t + 1) * inner]
        piece[freq_start:, :] = jnp.full((sub, inner), freqs[0], jnp.float32)


def start_kernel(wavefield, matrices, out, spectrum, turns):
    fill_y_turns(turns)

    def read(here, a):
        columns = slice(a * inner, (a + 1) * inner)
        return wavefield[0, 0, here, columns], wavefield[1, 0, here, columns]

    def write(part, value):
        y, x, c = part // 8, part // 2 % 4, part % 2
        out[y, 4 * c + x] = value

    forward_y(read, write, spectrum, matrices, turns)


def combine_kernel(
    last,
    moved,
    weights,
    back_matrices,
    matrices,
    out,
    fields,
    summed,
    spectrum,
    turns,
):
    fill_y_turns(turns)
    turn_cos, turn_sin = turns[0], turns[1]
    matrix = (back_matrices[0], back_matrices[1])
    for branch in range(2):
        for k in range(0, outer, 4):
            block = jnp.concatenate(
                [
                    jnp.concatenate([moved[2 * n, branch], moved[2 * n + 1, branch]], axis=1)
                    for n in range(k, k + 4)
                ],
                axis=0,
            )
            result = mix(cut(block), matrix)
            fields[branch, k : k + 4] = result.reshape(4, rows, 2 * inner)

    def back(c, carry):
        here = block_rows(c)
        for branch in range(2):
            values = []
            for k in range(outer):
                value = (fields[branch, k, here, :inner], fields[branch, k, here, inner:])
                turn = (turn_cos[k : k + 1, :], turn_sin[k : k + 1, :])
                values.append(value if k == 0 else times(value, turn))
            values = dft(values, 1)
            for a in range(outer):
                weight = (weights[2 * branch, a, here, :], weights[2 * branch + 1, a, here, :])
                value = times(values[a], weight)
                if branch == 1:
                    value = plus(value, (summed[0, a, here, :], summed[1, a, here, :]))
                if last and branch == 1:
                    columns = slice(a * inner, (a + 1) * inner)
                    inside = pl.ds(pl.multiple_of(c % 2 * sub, sub), sub)
                    out[c // 2, 0, inside, columns] = value[0]
                    out[c // 2, 1, inside, columns] = value[1]
                else:
                    summed[0, a, here, :] = value[0]
                    summed[1, a, here, :] = value[1]
        return carry

    lax.fori_loop(0, rows // sub, back, 0)
    if last:
        return

    def read(here, a):
        return summed[0, a, here, :], summed[1, a, here, :]

    def write(part, value):
        out[part] = value

    forward_y(read, write, spectrum, matrices, turns)


def weigh(level, place, freqs, ref_slow, tiles, weights):
    def full(value):
        return jnp.full((sub, inner), value, jnp.float32)

    lower, upper = full(ref_slow[level, 0]), full(ref_slow[level, 1])
    pace = depth_step * full(freqs[place[4]])
    inverse_gap = 1.0 / (upper - lower)
    turn = cis(pace * (lower - upper))

    z = 2 * place[0] + place[1]
    for n in range(ring):
        source = (z + n) % ring
        tile = tiles[n]

        def step(c, carry, source=source, tile=tile):
            from_y = (place[3] + 4 - c // 2) % 4
            here = pl.ds(pl.multiple_of(source // 2 * quarter + c % 2 * sub, sub), sub)
            for t in range(2):
                first = (2 * level + t) * quarter + c % 2 * sub
                slowness = 1.0 / tile[c // 2, pl.ds(pl.multiple_of(first, sub), sub), :]
                excess = slowness - lower
                upper_weight = jnp.clip(excess * inverse_gap, 0.0, 1.0)
                lower_weight = 1.0 - upper_weight
                phase = cis(pace * excess)
                other = times(phase, turn)
                a = 2 * (source % 2 * 4 + from_y) + t
                weights[0, a, here, :] = lower_weight * phase[0]
                weights[1, a, here, :] = lower_weight * phase[1]
                weights[2, a, here, :] = upper_weight * other[0]
                weights[3, a, here, :] = upper_weight * other[1]
            return carry

        lax.fori_loop(0, 8, step, 0, unroll=2)


def propagators(level, place, freqs, ref_slow):
    lane = lax.broadcasted_iota(jnp.int32, (sub, inner), 1)
    sub_row = lax.broadcasted_iota(jnp.int32, (sub, inner), 0)
    fy = folded(place[2] // 2 + outer * (half * (place[2] % 2) + lane % half))
    fy = fy * fy
    squares = []
    for branch in range(2):
        wave = jnp.full((sub, inner), freqs[place[4]]) * jnp.full((sub, inner), ref_slow[level, branch])
        squares.append(wave * wave)

    def at(c, k):
        fx = folded(2 * k + jnp.where(lane < half, 0, 1) + outer * (c * sub + sub_row))
        square = fx * fx + fy
        shifts = []
        for branch in range(2):
            target = squares[branch] - square
            cycles = depth_step * jnp.sqrt(jnp.abs(target))
            cosine, sine = cis(cycles)
            live = target >= 0
            shifts.append(
                (
                    jnp.where(live, cosine, jnp.exp(-two_pi * cycles)),
                    jnp.where(live, sine, 0.0),
                )
            )
        return shifts

    return at


def tables_kernel(place, freqs, ref_slow, *refs):
    tiles, tables, weights = refs[:ring], refs[ring : ring + depth], refs[ring + depth :]
    for level in range(depth):
        at = propagators(level, place, freqs, ref_slow)

        def step(c, carry, at=at, table=tables[level]):
            here = block_rows(c)
            second_half = pl.ds(pl.multiple_of(inner + c * sub, sub), sub)
            for k in range(outer // 2):
                columns = slice(k * inner, (k + 1) * inner)
                for branch, factor in enumerate(at(c, k)):
                    table[branch, here, columns] = factor[0]
                    table[branch, second_half, columns] = factor[1]
            return carry

        lax.fori_loop(0, inner // sub, step, 0)
        weigh(level, place, freqs, ref_slow, tiles, weights[level])


def slab_rows(a, top, c):
    return ((a // 4 * 2 + top) * 4 + a % 4) * rows + c * sub


def plane_chunk(a, top, c):
    return c // 2 * 8 + a % 4 * 2 + top, a // 4 * quarter + c % 2 * sub


def plane_rows(a, top, c):
    chunk, row = plane_chunk(a, top, c)
    return chunk * rows + row


def shift_kernel(
    rows_of,
    arrived,
    table,
    there_matrices,
    back_matrices,
    turns,
    out,
    spectrum,
    shifted,
    lane_turn,
):
    fill_lane_turns(lane_turn)
    lane = lax.broadcasted_iota(jnp.int32, (sub, inner), 1)
    low_lanes = lane < half
    groups = outer // 2
    steps = inner // sub

    def there(top, c, carry):
        position = top * half + c * sub
        here = pl.ds(pl.multiple_of(position, sub), sub)
        second_half = pl.ds(pl.multiple_of(inner + position, sub), sub)
        values = []
        for a in range(groups):
            first = arrived[pl.ds(pl.multiple_of(rows_of(a, top, c), sub), sub), :]
            second = arrived[pl.ds(pl.multiple_of(rows_of(a + groups, top, c), sub), sub), :]
            total, differ = first + second, first - second
            value = (
                jnp.where(low_lanes, total, pltpu.roll(differ, half, 1)),
                jnp.where(low_lanes, pltpu.roll(total, half, 1), differ),
            )
            turn = (lane_turn[0, a : a + 1, :], lane_turn[1, a : a + 1, :])
            values.append(value if a == 0 else times_conj(value, turn))
        values = dft(values, -1)
        for k in range(groups):
            value = times_conj(values[k], (turns[0, k, here, :], turns[1, k, here, :]))
            columns = slice(k * inner, (k + 1) * inner)
            spectrum[here, columns] = value[0]
            spectrum[second_half, columns] = value[1]
        return carry

    for top in range(2):
        lax.fori_loop(0, half // sub, functools.partial(there, top), 0)
    matrix = (there_matrices[0], there_matrices[1])
    for n in range(4):
        columns = slice(n * 2 * inner, (n + 1) * 2 * inner)
        spectrum[:, columns] = mix(matrix, cut(spectrum[:, columns]))

    def propagate(c, carry):
        here = block_rows(c)
        second_half = pl.ds(pl.multiple_of(inner + c * sub, sub), sub)
        for k in range(groups):
            columns = slice(k * inner, (k + 1) * inner)
            value = (spectrum[here, columns], spectrum[second_half, columns])
            for branch in range(2):
                moved = times(value, (table[branch, here, columns], table[branch, second_half, columns]))
                shifted[branch, here, columns] = moved[0]
                shifted[branch, second_half, columns] = moved[1]
        return carry

    lax.fori_loop(0, steps, propagate, 0)
    matrix = (back_matrices[0], back_matrices[1])
    for branch in range(2):
        for n in range(4):
            columns = slice(n * 2 * inner, (n + 1) * 2 * inner)
            shifted[branch, :, columns] = mix(matrix, cut(shifted[branch, :, columns]))

    for top in range(2):

        def back(c, carry, top=top):
            position = top * half + c * sub
            here = pl.ds(pl.multiple_of(position, sub), sub)
            second_half = pl.ds(pl.multiple_of(inner + position, sub), sub)
            for branch in range(2):
                values = []
                for k in range(groups):
                    columns = slice(k * inner, (k + 1) * inner)
                    value = (shifted[branch, here, columns], shifted[branch, second_half, columns])
                    values.append(times(value, (turns[0, k, here, :], turns[1, k, here, :])))
                values = dft(values, 1)
                for a in range(groups):
                    value = values[a]
                    if a > 0:
                        value = times(value, (lane_turn[0, a : a + 1, :], lane_turn[1, a : a + 1, :]))
                    even = jnp.where(low_lanes, value[0], pltpu.roll(value[1], half, 1))
                    odd = jnp.where(low_lanes, pltpu.roll(value[0], half, 1), value[1])
                    for at, result in ((a, even + odd), (a + groups, even - odd)):
                        chunk, row = plane_chunk(at, top, c)
                        out[chunk, branch, pl.ds(pl.multiple_of(row, sub), sub), :] = result
            return carry

        lax.fori_loop(0, half // sub, back, 0)


def call(kernel, shapes, scratch, scalars, operands):
    vmem = pl.BlockSpec(memory_space=pltpu.VMEM)
    smem = pl.BlockSpec(memory_space=pltpu.SMEM)
    return pl.pallas_call(
        kernel,
        out_shape=[jax.ShapeDtypeStruct(s, jnp.float32) for s in shapes],
        in_specs=[smem] * len(scalars) + [vmem] * len(operands),
        out_specs=[vmem] * len(shapes),
        scratch_shapes=[pltpu.VMEM(s, jnp.float32) for s in scratch],
        compiler_params=pltpu.CompilerParams(vmem_limit_bytes=28 * 1024 * 1024),
    )(*scalars, *operands)


def exchange(values, axes):
    return lax.all_to_all(values, axes, split_axis=0, concat_axis=0, tiled=True)


def around_z(tile):
    axes = ("zl", "zh")
    index = [n % 2 * 4 + n // 2 for n in range(ring)]
    down = [(index[n], index[n - 1]) for n in range(ring)]
    up = [(index[n - 1], index[n]) for n in range(ring)]
    tiles = [tile] + [None] * (ring - 1)
    above = below = tile
    for n in range(1, 5):
        above = lax.ppermute(above, axes, down)
        tiles[n] = above
        if n < 4:
            below = lax.ppermute(below, axes, up)
            tiles[ring - n] = below
    return tiles


def shards(wavefield, freqs, velocity, ref_slow):
    zh, zl, y = lax.axis_index("zh"), lax.axis_index("zl"), lax.axis_index("y")
    part = (y * 4 + lax.axis_index("x")) * 2 + lax.axis_index("c")
    place = jnp.stack([zh, zl, part, y, (y + 4 - zh) % 4])

    fy_matrix = np.stack(forward_y_matrix())
    iy_matrix = np.stack(inverse_y_matrix())
    fx_matrix = np.stack(x_matrix(-1))
    ix_matrix = np.stack(x_matrix(1))
    turn_x = np.stack(x_turns())

    plane = ("y", "x", "c")
    packed = (parts, rows, inner)
    spectrum_shape = (outer, rows, 2 * inner)
    y_turns_shape = (2, outer, inner)
    folded_shape = (2 * inner, length // 2)

    pieces = call(carve_kernel, [(message, inner)] * 4, [], (place, freqs), (velocity,))
    pieces = [
        lax.ppermute(piece, "y", [(m, (m + n) % 4) for m in range(4)]) if n else piece
        for n, piece in enumerate(pieces)
    ]
    tile = jnp.stack(pieces)
    tiles = around_z(tile)
    common = (place, tile[:, freq_start, 0], ref_slow)
    (sent,) = call(
        start_kernel,
        [(4, 8, rows, inner)],
        [spectrum_shape, y_turns_shape],
        (),
        (wavefield, fy_matrix),
    )
    sent = exchange(sent, ("y",)).reshape(packed)
    sent, *tiles = lax.optimization_barrier((sent, *tiles))
    arrived = exchange(sent, ("zh", "c", "x"))
    tables = call(
        tables_kernel,
        [(2, *folded_shape)] * depth + [(4, outer, rows, inner)] * depth,
        [],
        common,
        tiles,
    )
    for level in range(depth):
        if level:
            arrived = exchange(sent, plane)
        (shifted,) = call(
            functools.partial(shift_kernel, plane_rows if level else slab_rows),
            [(parts, 2, rows, inner)],
            [folded_shape, (2, *folded_shape), (2, outer // 2, inner)],
            (),
            (arrived.reshape(length, inner), tables[level], fx_matrix, ix_matrix, turn_x),
        )
        moved = exchange(shifted, plane)
        last = level == depth - 1
        (sent,) = call(
            functools.partial(combine_kernel, last),
            [(4, 2, quarter, length) if last else packed],
            [(2, *spectrum_shape), (2, outer, rows, inner), spectrum_shape, y_turns_shape],
            (),
            (moved, tables[depth + level], iy_matrix, fy_matrix),
        )
    back = exchange(exchange(sent, ("zh",)), ("y",))
    return back.transpose(1, 0, 2, 3).reshape(2, 1, rows, length)


def solution(mesh):
    axes = ("zl", "y", "zh", "x", "c")
    return jax.shard_map(
        shards,
        mesh=Mesh(mesh.devices.reshape(2, 4, 4, 4, 2), axes),
        in_specs=(
            P(None, axes[:2], axes[2:], None),
            P(axes[:2]),
            P(None, axes[2:], axes[:2]),
            P(),
        ),
        out_specs=P(None, axes[:2], axes[2:], None),
        check_vma=False,
    )
```

```python
import functools
import math

import jax
import jax.numpy as jnp
import numpy as np
from jax import lax
from jax.experimental import pallas as pl
from jax.experimental.pallas import tpu as pltpu
from jax.sharding import Mesh
from jax.sharding import PartitionSpec as P

two_pi = 2.0 * math.pi
depth_step = 2.0

length = 2048
outer = 16
inner = 128
half = 64
rows = 64
parts = 32
sub = 8
depth = 3
ring = 8
quarter = 16
level_rows = 2 * quarter
cell_start = 8 * rows
freq_start = cell_start + depth * level_rows
message = freq_start + sub


def split_bf16(matrix):
    matrix = np.asarray(matrix, np.float32)
    high = matrix.astype(jnp.bfloat16)
    low = (matrix - high.astype(np.float32)).astype(jnp.bfloat16)
    return high, low


def dft_inner(sign):
    index = np.arange(inner)
    angle = sign * two_pi / inner * (index[:, None] * index[None, :] % inner)
    scale = 1.0 / math.sqrt(length)
    return np.cos(angle) * scale, np.sin(angle) * scale


def packed_order():
    low = np.arange(half)
    return np.concatenate([low, inner + low, half + low, inner + half + low])


def forward_y_matrix():
    real, imag = dft_inner(-1)
    full = np.block([[real, imag], [-imag, real]])
    return split_bf16(full[:, packed_order()])


def inverse_y_matrix():
    real, imag = dft_inner(1)
    full = np.block([[real, imag], [-imag, real]])
    return split_bf16(full[packed_order(), :])


def x_matrix(sign):
    real, imag = dft_inner(sign)
    return split_bf16(np.block([[real, -imag], [imag, real]]))


def x_turns():
    upper = (np.arange(inner) >= half).astype(np.int64)
    k = 2 * np.arange(outer // 2)[:, None, None] + upper[None, None, :]
    angle = two_pi / length * (k * np.arange(inner)[None, :, None])
    return np.cos(angle).astype(np.float32), np.sin(angle).astype(np.float32)


def fit_even(function, terms):
    nodes = np.cos(np.pi * (np.arange(256) + 0.5) / 256)
    basis = np.stack([nodes ** (2 * n) for n in range(terms)], axis=1)
    solved = np.linalg.lstsq(basis, function(nodes), rcond=None)[0]
    return [float(c) for c in solved]


cos_fit = fit_even(lambda z: np.cos(np.pi * z), 9)
sin_fit = fit_even(lambda z: np.pi * np.sinc(z), 9)


def cis(cycles):
    z = 2.0 * (cycles - jnp.floor(cycles + 0.5))
    square = z * z
    cosine = cos_fit[-1]
    for c in cos_fit[-2::-1]:
        cosine = cosine * square + c
    sine = sin_fit[-1]
    for c in sin_fit[-2::-1]:
        sine = sine * square + c
    return cosine, sine * z


def fill_y_turns(turns):
    k = lax.broadcasted_iota(jnp.int32, (outer, inner), 0)
    b = lax.broadcasted_iota(jnp.int32, (outer, inner), 1)
    turns[0], turns[1] = cis((k * b).astype(jnp.float32) * (1.0 / length))


def fill_lane_turns(turns):
    a = lax.broadcasted_iota(jnp.int32, (outer // 2, inner), 0)
    lane = lax.broadcasted_iota(jnp.int32, (outer // 2, inner), 1)
    turns[0], turns[1] = cis(jnp.where(lane < half, 0, a).astype(jnp.float32) * (1.0 / outer))


def times(a, b):
    return (a[0] * b[0] - a[1] * b[1], a[0] * b[1] + a[1] * b[0])


def times_conj(a, b):
    return (a[0] * b[0] + a[1] * b[1], a[1] * b[0] - a[0] * b[1])


def plus(a, b):
    return (a[0] + b[0], a[1] + b[1])


def minus(a, b):
    return (a[0] - b[0], a[1] - b[1])


def times_root(a, power, n, sign):
    eighth = (8 * power) % (8 * n)
    real, imag = a
    if eighth % n == 0:
        step = (eighth // n) % 8
        if sign < 0:
            step = (8 - step) % 8
        if step == 0:
            return a
        if step == 2:
            return (-imag, real)
        if step == 4:
            return (-real, -imag)
        if step == 6:
            return (imag, -real)
        root = math.sqrt(0.5)
        total = (real + imag) * root
        differ = (real - imag) * root
        if step == 1:
            return (differ, total)
        if step == 3:
            return (-total, differ)
        if step == 5:
            return (-differ, -total)
        return (total, -differ)
    angle = sign * two_pi * power / n
    c, s = math.cos(angle), math.sin(angle)
    return (real * c - imag * s, real * s + imag * c)


def dft(values, sign):
    n = len(values)
    if n == 2:
        return [plus(*values), minus(*values)]
    if n == 4:
        t0, t1 = plus(values[0], values[2]), minus(values[0], values[2])
        t2, t3 = plus(values[1], values[3]), minus(values[1], values[3])
        if sign > 0:
            y1 = (t1[0] - t3[1], t1[1] + t3[0])
            y3 = (t1[0] + t3[1], t1[1] - t3[0])
        else:
            y1 = (t1[0] + t3[1], t1[1] - t3[0])
            y3 = (t1[0] - t3[1], t1[1] + t3[0])
        return [plus(t0, t2), y1, minus(t0, t2), y3]
    radix = 2 if n == 8 else 4
    m = n // radix
    inside = [dft(values[s::radix], sign) for s in range(radix)]
    out = [None] * n
    for k in range(m):
        turned = [times_root(inside[s][k], s * k, n, sign) for s in range(radix)]
        for step, value in enumerate(dft(turned, sign)):
            out[k + m * step] = value
    return out


def cut(x):
    high = x.astype(jnp.bfloat16)
    low = (x - high.astype(jnp.float32)).astype(jnp.bfloat16)
    return high, low


def product(a, b):
    return jnp.dot(a, b, preferred_element_type=jnp.float32)


def mix(a, b):
    (a_high, a_low), (b_high, b_low) = a, b
    return product(a_high, b_high) + (product(a_high, b_low) + product(a_low, b_high))


def folded(number):
    return jnp.minimum(number, length - number).astype(jnp.float32) * (1.0 / length)


def block_rows(step):
    return pl.ds(pl.multiple_of(step * sub, sub), sub)


def forward_y(read, write, spectrum, matrices, turns):
    turn_cos, turn_sin = turns[0], turns[1]

    def step(c, carry):
        here = block_rows(c)
        values = dft([read(here, a) for a in range(outer)], -1)
        for k in range(outer):
            turn = (turn_cos[k : k + 1, :], turn_sin[k : k + 1, :])
            value = values[k] if k == 0 else times_conj(values[k], turn)
            spectrum[k, here, :inner] = value[0]
            spectrum[k, here, inner:] = value[1]
        return carry

    lax.fori_loop(0, rows // sub, step, 0)
    matrix = (matrices[0], matrices[1])
    for k in range(0, outer, 4):
        block = spectrum[k : k + 4].reshape(4 * rows, 2 * inner)
        result = mix(cut(block), matrix)
        for n in range(4):
            one = result[n * rows : (n + 1) * rows]
            write(2 * (k + n), one[:, :inner])
            write(2 * (k + n) + 1, one[:, inner:])


def start_kernel(freqs, wavefield, velocity, matrices, out, spectrum, turns):
    fill_y_turns(turns)

    def read(here, a):
        columns = slice(a * inner, (a + 1) * inner)
        return wavefield[0, 0, here, columns], wavefield[1, 0, here, columns]

    def write(part, value):
        y, x, c = part // 8, part // 2 % 4, part % 2
        place = (4 * c + x) * rows
        out[y, place : place + rows, :] = value

    forward_y(read, write, spectrum, matrices, turns)
    for y in range(4):
        for level in range(depth):
            for t in range(2):
                place = cell_start + (2 * level + t) * quarter
                out[y, place : place + quarter, :] = velocity[
                    level, y * quarter : (y + 1) * quarter, t * inner : (t + 1) * inner
                ]
        out[y, freq_start:, :] = jnp.full((sub, inner), freqs[0], jnp.float32)


def combine_kernel(
    last,
    moved,
    weights,
    back_matrices,
    matrices,
    out,
    fields,
    summed,
    spectrum,
    turns,
):
    fill_y_turns(turns)
    turn_cos, turn_sin = turns[0], turns[1]
    matrix = (back_matrices[0], back_matrices[1])
    for branch in range(2):
        for k in range(0, outer, 4):
            block = jnp.concatenate(
                [
                    jnp.concatenate([moved[2 * n, branch], moved[2 * n + 1, branch]], axis=1)
                    for n in range(k, k + 4)
                ],
                axis=0,
            )
            result = mix(cut(block), matrix)
            fields[branch, k : k + 4] = result.reshape(4, rows, 2 * inner)

    def back(c, carry):
        here = block_rows(c)
        for branch in range(2):
            values = []
            for k in range(outer):
                value = (fields[branch, k, here, :inner], fields[branch, k, here, inner:])
                turn = (turn_cos[k : k + 1, :], turn_sin[k : k + 1, :])
                values.append(value if k == 0 else times(value, turn))
            values = dft(values, 1)
            for a in range(outer):
                weight = (weights[2 * branch, a, here, :], weights[2 * branch + 1, a, here, :])
                value = times(values[a], weight)
                if branch == 1:
                    value = plus(value, (summed[0, a, here, :], summed[1, a, here, :]))
                if last and branch == 1:
                    columns = slice(a * inner, (a + 1) * inner)
                    inside = pl.ds(pl.multiple_of(c % 2 * sub, sub), sub)
                    out[c // 2, 0, inside, columns] = value[0]
                    out[c // 2, 1, inside, columns] = value[1]
                else:
                    summed[0, a, here, :] = value[0]
                    summed[1, a, here, :] = value[1]
        return carry

    lax.fori_loop(0, rows // sub, back, 0)
    if last:
        return

    def read(here, a):
        return summed[0, a, here, :], summed[1, a, here, :]

    def write(part, value):
        out[part] = value

    forward_y(read, write, spectrum, matrices, turns)


def weigh(level, first_level, place, freqs, ref_slow, tiles, weights):
    def full(value):
        return jnp.full((sub, inner), value, jnp.float32)

    lower, upper = full(ref_slow[level, 0]), full(ref_slow[level, 1])
    pace = depth_step * full(freqs[place[0]])
    inverse_gap = 1.0 / (upper - lower)
    turn = cis(pace * (lower - upper))

    z = 2 * place[0] + place[1]
    for n in range(ring):
        source = (z + n) % ring
        tile = tiles[n]

        def step(c, carry, source=source, tile=tile):
            from_y = c // 2
            here = pl.ds(pl.multiple_of(source // 2 * quarter + c % 2 * sub, sub), sub)
            for t in range(2):
                first = (2 * (level - first_level) + t) * quarter + c % 2 * sub
                slowness = 1.0 / tile[from_y, pl.ds(pl.multiple_of(first, sub), sub), :]
                excess = slowness - lower
                upper_weight = jnp.clip(excess * inverse_gap, 0.0, 1.0)
                lower_weight = 1.0 - upper_weight
                phase = cis(pace * excess)
                other = times(phase, turn)
                a = 2 * (source % 2 * 4 + from_y) + t
                weights[0, a, here, :] = lower_weight * phase[0]
                weights[1, a, here, :] = lower_weight * phase[1]
                weights[2, a, here, :] = upper_weight * other[0]
                weights[3, a, here, :] = upper_weight * other[1]
            return carry

        lax.fori_loop(0, 8, step, 0, unroll=2)


def propagators(level, place, freqs, ref_slow):
    lane = lax.broadcasted_iota(jnp.int32, (sub, inner), 1)
    sub_row = lax.broadcasted_iota(jnp.int32, (sub, inner), 0)
    fy = folded(place[2] // 2 + outer * (half * (place[2] % 2) + lane % half))
    fy = fy * fy
    squares = []
    for branch in range(2):
        wave = jnp.full((sub, inner), freqs[place[0]]) * jnp.full((sub, inner), ref_slow[level, branch])
        squares.append(wave * wave)

    def at(c, k):
        fx = folded(2 * k + jnp.where(lane < half, 0, 1) + outer * (c * sub + sub_row))
        square = fx * fx + fy
        shifts = []
        for branch in range(2):
            target = squares[branch] - square
            cycles = depth_step * jnp.sqrt(jnp.abs(target))
            cosine, sine = cis(cycles)
            live = target >= 0
            shifts.append(
                (
                    jnp.where(live, cosine, jnp.exp(-two_pi * cycles)),
                    jnp.where(live, sine, 0.0),
                )
            )
        return shifts

    return at


def propagator_kernel(place, freqs, ref_slow, *tables):
    for level, table in enumerate(tables):
        at = propagators(level, place, freqs, ref_slow)

        def step(c, carry, at=at, table=table):
            here = block_rows(c)
            second_half = pl.ds(pl.multiple_of(inner + c * sub, sub), sub)
            for k in range(outer // 2):
                columns = slice(k * inner, (k + 1) * inner)
                for branch, factor in enumerate(at(c, k)):
                    table[branch, here, columns] = factor[0]
                    table[branch, second_half, columns] = factor[1]
            return carry

        lax.fori_loop(0, inner // sub, step, 0)


def weigh_kernel(first_level, place, freqs, ref_slow, *refs):
    tiles = refs[:ring]
    for n, weights in enumerate(refs[ring:]):
        weigh(first_level + n, first_level, place, freqs, ref_slow, tiles, weights)


def slab_rows(a, top, c):
    return ((a // 4 * 2 + top) * 4 + a % 4) * rows + c * sub


def plane_chunk(a, top, c):
    return c // 2 * 8 + a % 4 * 2 + top, a // 4 * quarter + c % 2 * sub


def plane_rows(a, top, c):
    chunk, row = plane_chunk(a, top, c)
    return chunk * rows + row


def shift_kernel(
    rows_of,
    arrived,
    table,
    there_matrices,
    back_matrices,
    turns,
    out,
    spectrum,
    shifted,
    lane_turn,
):
    fill_lane_turns(lane_turn)
    lane = lax.broadcasted_iota(jnp.int32, (sub, inner), 1)
    low_lanes = lane < half
    groups = outer // 2
    steps = inner // sub

    def there(top, c, carry):
        position = top * half + c * sub
        here = pl.ds(pl.multiple_of(position, sub), sub)
        second_half = pl.ds(pl.multiple_of(inner + position, sub), sub)
        values = []
        for a in range(groups):
            first = arrived[pl.ds(pl.multiple_of(rows_of(a, top, c), sub), sub), :]
            second = arrived[pl.ds(pl.multiple_of(rows_of(a + groups, top, c), sub), sub), :]
            total, differ = first + second, first - second
            value = (
                jnp.where(low_lanes, total, pltpu.roll(differ, half, 1)),
                jnp.where(low_lanes, pltpu.roll(total, half, 1), differ),
            )
            turn = (lane_turn[0, a : a + 1, :], lane_turn[1, a : a + 1, :])
            values.append(value if a == 0 else times_conj(value, turn))
        values = dft(values, -1)
        for k in range(groups):
            value = times_conj(values[k], (turns[0, k, here, :], turns[1, k, here, :]))
            columns = slice(k * inner, (k + 1) * inner)
            spectrum[here, columns] = value[0]
            spectrum[second_half, columns] = value[1]
        return carry

    for top in range(2):
        lax.fori_loop(0, half // sub, functools.partial(there, top), 0)
    matrix = (there_matrices[0], there_matrices[1])
    for n in range(4):
        columns = slice(n * 2 * inner, (n + 1) * 2 * inner)
        spectrum[:, columns] = mix(matrix, cut(spectrum[:, columns]))

    def propagate(c, carry):
        here = block_rows(c)
        second_half = pl.ds(pl.multiple_of(inner + c * sub, sub), sub)
        for k in range(groups):
            columns = slice(k * inner, (k + 1) * inner)
            value = (spectrum[here, columns], spectrum[second_half, columns])
            for branch in range(2):
                moved = times(value, (table[branch, here, columns], table[branch, second_half, columns]))
                shifted[branch, here, columns] = moved[0]
                shifted[branch, second_half, columns] = moved[1]
        return carry

    lax.fori_loop(0, steps, propagate, 0)
    matrix = (back_matrices[0], back_matrices[1])
    for branch in range(2):
        for n in range(4):
            columns = slice(n * 2 * inner, (n + 1) * 2 * inner)
            shifted[branch, :, columns] = mix(matrix, cut(shifted[branch, :, columns]))

    for top in range(2):

        def back(c, carry, top=top):
            position = top * half + c * sub
            here = pl.ds(pl.multiple_of(position, sub), sub)
            second_half = pl.ds(pl.multiple_of(inner + position, sub), sub)
            for branch in range(2):
                values = []
                for k in range(groups):
                    columns = slice(k * inner, (k + 1) * inner)
                    value = (shifted[branch, here, columns], shifted[branch, second_half, columns])
                    values.append(times(value, (turns[0, k, here, :], turns[1, k, here, :])))
                values = dft(values, 1)
                for a in range(groups):
                    value = values[a]
                    if a > 0:
                        value = times(value, (lane_turn[0, a : a + 1, :], lane_turn[1, a : a + 1, :]))
                    even = jnp.where(low_lanes, value[0], pltpu.roll(value[1], half, 1))
                    odd = jnp.where(low_lanes, pltpu.roll(value[0], half, 1), value[1])
                    for at, result in ((a, even + odd), (a + groups, even - odd)):
                        chunk, row = plane_chunk(at, top, c)
                        out[chunk, branch, pl.ds(pl.multiple_of(row, sub), sub), :] = result
            return carry

        lax.fori_loop(0, half // sub, back, 0)


def call(kernel, shapes, scratch, scalars, operands):
    vmem = pl.BlockSpec(memory_space=pltpu.VMEM)
    smem = pl.BlockSpec(memory_space=pltpu.SMEM)
    return pl.pallas_call(
        kernel,
        out_shape=[jax.ShapeDtypeStruct(s, jnp.float32) for s in shapes],
        in_specs=[smem] * len(scalars) + [vmem] * len(operands),
        out_specs=[vmem] * len(shapes),
        scratch_shapes=[pltpu.VMEM(s, jnp.float32) for s in scratch],
        compiler_params=pltpu.CompilerParams(vmem_limit_bytes=12 * 1024 * 1024),
    )(*scalars, *operands)


def exchange(values, axes):
    return lax.all_to_all(values, axes, split_axis=0, concat_axis=0, tiled=True)


def around_z(tile):
    axes = ("zl", "zh")
    index = [n % 2 * 4 + n // 2 for n in range(ring)]
    down = [(index[n], index[n - 1]) for n in range(ring)]
    up = [(index[n - 1], index[n]) for n in range(ring)]
    tiles = [tile] + [None] * (ring - 1)
    above = below = tile
    for n in range(1, 5):
        above = lax.ppermute(above, axes, down)
        tiles[n] = above
        if n < 4:
            below = lax.ppermute(below, axes, up)
            tiles[ring - n] = below
    return tiles


def shards(wavefield, freqs, velocity, ref_slow):
    zh, zl = lax.axis_index("zh"), lax.axis_index("zl")
    part = (lax.axis_index("y") * 4 + lax.axis_index("x")) * 2 + lax.axis_index("c")
    place = jnp.stack([zh, zl, part])

    fy_matrix = np.stack(forward_y_matrix())
    iy_matrix = np.stack(inverse_y_matrix())
    fx_matrix = np.stack(x_matrix(-1))
    ix_matrix = np.stack(x_matrix(1))
    turn_x = np.stack(x_turns())

    plane = ("y", "x", "c")
    packed = (parts, rows, inner)
    spectrum_shape = (outer, rows, 2 * inner)
    y_turns_shape = (2, outer, inner)
    folded_shape = (2 * inner, length // 2)

    (sent,) = call(
        start_kernel,
        [(4, message, inner)],
        [spectrum_shape, y_turns_shape],
        (freqs,),
        (wavefield, velocity, fy_matrix),
    )
    sent = exchange(sent, ("y",))
    sent, cells = lax.optimization_barrier((sent[:, :cell_start], sent[:, cell_start:]))
    common = (place, cells[:, -1, 0], ref_slow)
    first_tile = cells[:, :level_rows]
    later_tile = cells[:, level_rows : depth * level_rows]
    arrived = exchange(sent.reshape(packed), ("zh", "c", "x"))
    tables = call(propagator_kernel, [(2, *folded_shape)] * depth, [], common, ())
    weights = []
    for level in range(depth):
        if level:
            arrived = exchange(sent, plane)
        if level == 0:
            arrived, first_tile, later_tile = lax.optimization_barrier(
                (arrived, first_tile, later_tile)
            )
            tiles = around_z(first_tile)
        if level == 1:
            arrived, later_tile = lax.optimization_barrier((arrived, later_tile))
            tiles = around_z(later_tile)
        if level < 2:
            weights += call(
                functools.partial(weigh_kernel, level),
                [(4, outer, rows, inner)] * (depth - 1 if level else 1),
                [],
                common,
                tiles,
            )
        (shifted,) = call(
            functools.partial(shift_kernel, plane_rows if level else slab_rows),
            [(parts, 2, rows, inner)],
            [folded_shape, (2, *folded_shape), (2, outer // 2, inner)],
            (),
            (arrived.reshape(length, inner), tables[level], fx_matrix, ix_matrix, turn_x),
        )
        moved = exchange(shifted, plane)
        last = level == depth - 1
        (sent,) = call(
            functools.partial(combine_kernel, last),
            [(4, 2, quarter, length) if last else packed],
            [(2, *spectrum_shape), (2, outer, rows, inner), spectrum_shape, y_turns_shape],
            (),
            (moved, weights[level], iy_matrix, fy_matrix),
        )
    back = exchange(exchange(sent, ("zh",)), ("y",))
    return back.transpose(1, 0, 2, 3).reshape(2, 1, rows, length)


def solution(mesh):
    axes = ("zl", "y", "zh", "x", "c")
    return jax.shard_map(
        shards,
        mesh=Mesh(mesh.devices.reshape(2, 4, 4, 4, 2), axes),
        in_specs=(
            P(None, axes[:2], axes[2:], None),
            P(axes[:2]),
            P(None, axes[2:], axes[:2]),
            P(),
        ),
        out_specs=P(None, axes[:2], axes[2:], None),
        check_vma=False,
    )
```

```python
import functools
import math

import jax
import jax.numpy as jnp
import numpy as np
from jax import lax
from jax.experimental import pallas as pl
from jax.experimental.pallas import tpu as pltpu
from jax.sharding import Mesh
from jax.sharding import PartitionSpec as P

two_pi = 2.0 * math.pi
depth_step = 2.0

length = 2048
outer = 16
inner = 128
half = 64
rows = 64
parts = 32
sub = 8
depth = 3
ring = 8
quarter = 16
level_rows = 2 * quarter
cell_start = 8 * rows
freq_start = cell_start + depth * level_rows
message = freq_start + sub


def split_bf16(matrix):
    matrix = np.asarray(matrix, np.float32)
    high = matrix.astype(jnp.bfloat16)
    low = (matrix - high.astype(np.float32)).astype(jnp.bfloat16)
    return high, low


def dft_inner(sign):
    index = np.arange(inner)
    angle = sign * two_pi / inner * (index[:, None] * index[None, :] % inner)
    scale = 1.0 / math.sqrt(length)
    return np.cos(angle) * scale, np.sin(angle) * scale


def packed_order():
    low = np.arange(half)
    return np.concatenate([low, inner + low, half + low, inner + half + low])


def forward_y_matrix():
    real, imag = dft_inner(-1)
    full = np.block([[real, imag], [-imag, real]])
    return split_bf16(full[:, packed_order()])


def inverse_y_matrix():
    real, imag = dft_inner(1)
    full = np.block([[real, imag], [-imag, real]])
    return split_bf16(full[packed_order(), :])


def x_matrix(sign):
    real, imag = dft_inner(sign)
    return split_bf16(np.block([[real, -imag], [imag, real]]))


def x_turns():
    upper = (np.arange(inner) >= half).astype(np.int64)
    k = 2 * np.arange(outer // 2)[:, None, None] + upper[None, None, :]
    angle = two_pi / length * (k * np.arange(inner)[None, :, None])
    return np.cos(angle).astype(np.float32), np.sin(angle).astype(np.float32)


def fit_even(function, terms):
    nodes = np.cos(np.pi * (np.arange(256) + 0.5) / 256)
    basis = np.stack([nodes ** (2 * n) for n in range(terms)], axis=1)
    solved = np.linalg.lstsq(basis, function(nodes), rcond=None)[0]
    return [float(c) for c in solved]


cos_fit = fit_even(lambda z: np.cos(np.pi * z), 9)
sin_fit = fit_even(lambda z: np.pi * np.sinc(z), 9)


def cis(cycles):
    z = 2.0 * (cycles - jnp.floor(cycles + 0.5))
    square = z * z
    cosine = cos_fit[-1]
    for c in cos_fit[-2::-1]:
        cosine = cosine * square + c
    sine = sin_fit[-1]
    for c in sin_fit[-2::-1]:
        sine = sine * square + c
    return cosine, sine * z


def fill_y_turns(turns):
    k = lax.broadcasted_iota(jnp.int32, (outer, inner), 0)
    b = lax.broadcasted_iota(jnp.int32, (outer, inner), 1)
    turns[0], turns[1] = cis((k * b).astype(jnp.float32) * (1.0 / length))


def fill_lane_turns(turns):
    a = lax.broadcasted_iota(jnp.int32, (outer // 2, inner), 0)
    lane = lax.broadcasted_iota(jnp.int32, (outer // 2, inner), 1)
    turns[0], turns[1] = cis(jnp.where(lane < half, 0, a).astype(jnp.float32) * (1.0 / outer))


def times(a, b):
    return (a[0] * b[0] - a[1] * b[1], a[0] * b[1] + a[1] * b[0])


def times_conj(a, b):
    return (a[0] * b[0] + a[1] * b[1], a[1] * b[0] - a[0] * b[1])


def plus(a, b):
    return (a[0] + b[0], a[1] + b[1])


def minus(a, b):
    return (a[0] - b[0], a[1] - b[1])


def times_root(a, power, n, sign):
    eighth = (8 * power) % (8 * n)
    real, imag = a
    if eighth % n == 0:
        step = (eighth // n) % 8
        if sign < 0:
            step = (8 - step) % 8
        if step == 0:
            return a
        if step == 2:
            return (-imag, real)
        if step == 4:
            return (-real, -imag)
        if step == 6:
            return (imag, -real)
        root = math.sqrt(0.5)
        total = (real + imag) * root
        differ = (real - imag) * root
        if step == 1:
            return (differ, total)
        if step == 3:
            return (-total, differ)
        if step == 5:
            return (-differ, -total)
        return (total, -differ)
    angle = sign * two_pi * power / n
    c, s = math.cos(angle), math.sin(angle)
    return (real * c - imag * s, real * s + imag * c)


def dft(values, sign):
    n = len(values)
    if n == 2:
        return [plus(*values), minus(*values)]
    if n == 4:
        t0, t1 = plus(values[0], values[2]), minus(values[0], values[2])
        t2, t3 = plus(values[1], values[3]), minus(values[1], values[3])
        if sign > 0:
            y1 = (t1[0] - t3[1], t1[1] + t3[0])
            y3 = (t1[0] + t3[1], t1[1] - t3[0])
        else:
            y1 = (t1[0] + t3[1], t1[1] - t3[0])
            y3 = (t1[0] - t3[1], t1[1] + t3[0])
        return [plus(t0, t2), y1, minus(t0, t2), y3]
    radix = 2 if n == 8 else 4
    m = n // radix
    inside = [dft(values[s::radix], sign) for s in range(radix)]
    out = [None] * n
    for k in range(m):
        turned = [times_root(inside[s][k], s * k, n, sign) for s in range(radix)]
        for step, value in enumerate(dft(turned, sign)):
            out[k + m * step] = value
    return out


def cut(x):
    high = x.astype(jnp.bfloat16)
    low = (x - high.astype(jnp.float32)).astype(jnp.bfloat16)
    return high, low


def product(a, b):
    return jnp.dot(a, b, preferred_element_type=jnp.float32)


def mix(a, b):
    (a_high, a_low), (b_high, b_low) = a, b
    left = jnp.concatenate([a_high, a_high, a_low], axis=1)
    right = jnp.concatenate([b_high, b_low, b_high], axis=0)
    return product(left, right)


def folded(number):
    return jnp.minimum(number, length - number).astype(jnp.float32) * (1.0 / length)


def block_rows(step):
    return pl.ds(pl.multiple_of(step * sub, sub), sub)


def forward_y(read, write, spectrum, matrices, turns):
    turn_cos, turn_sin = turns[0], turns[1]

    def step(c, carry):
        here = block_rows(c)
        values = dft([read(here, a) for a in range(outer)], -1)
        for k in range(outer):
            turn = (turn_cos[k : k + 1, :], turn_sin[k : k + 1, :])
            value = values[k] if k == 0 else times_conj(values[k], turn)
            spectrum[k, here, :inner] = value[0]
            spectrum[k, here, inner:] = value[1]
        return carry

    lax.fori_loop(0, rows // sub, step, 0)
    matrix = (matrices[0], matrices[1])
    for k in range(0, outer, 4):
        block = spectrum[k : k + 4].reshape(4 * rows, 2 * inner)
        result = mix(cut(block), matrix)
        for n in range(4):
            one = result[n * rows : (n + 1) * rows]
            write(2 * (k + n), one[:, :inner])
            write(2 * (k + n) + 1, one[:, inner:])


def start_kernel(freqs, wavefield, velocity, matrices, out, spectrum, turns):
    fill_y_turns(turns)

    def read(here, a):
        columns = slice(a * inner, (a + 1) * inner)
        return wavefield[0, 0, here, columns], wavefield[1, 0, here, columns]

    def write(part, value):
        y, x, c = part // 8, part // 2 % 4, part % 2
        place = (4 * c + x) * rows
        out[y, place : place + rows, :] = value

    forward_y(read, write, spectrum, matrices, turns)
    for y in range(4):
        for level in range(depth):
            for t in range(2):
                place = cell_start + (2 * level + t) * quarter
                out[y, place : place + quarter, :] = velocity[
                    level, y * quarter : (y + 1) * quarter, t * inner : (t + 1) * inner
                ]
        out[y, freq_start:, :] = jnp.full((sub, inner), freqs[0], jnp.float32)


def combine_kernel(
    last,
    moved,
    weights,
    back_matrices,
    matrices,
    out,
    fields,
    summed,
    spectrum,
    turns,
):
    fill_y_turns(turns)
    turn_cos, turn_sin = turns[0], turns[1]
    matrix = (back_matrices[0], back_matrices[1])
    for branch in range(2):
        for k in range(0, outer, 4):
            block = jnp.concatenate(
                [
                    jnp.concatenate([moved[2 * n, branch], moved[2 * n + 1, branch]], axis=1)
                    for n in range(k, k + 4)
                ],
                axis=0,
            )
            result = mix(cut(block), matrix)
            fields[branch, k : k + 4] = result.reshape(4, rows, 2 * inner)

    def back(c, carry):
        here = block_rows(c)
        for branch in range(2):
            values = []
            for k in range(outer):
                value = (fields[branch, k, here, :inner], fields[branch, k, here, inner:])
                turn = (turn_cos[k : k + 1, :], turn_sin[k : k + 1, :])
                values.append(value if k == 0 else times(value, turn))
            values = dft(values, 1)
            for a in range(outer):
                weight = (weights[2 * branch, a, here, :], weights[2 * branch + 1, a, here, :])
                value = times(values[a], weight)
                if branch == 1:
                    value = plus(value, (summed[0, a, here, :], summed[1, a, here, :]))
                if last and branch == 1:
                    columns = slice(a * inner, (a + 1) * inner)
                    inside = pl.ds(pl.multiple_of(c % 2 * sub, sub), sub)
                    out[c // 2, 0, inside, columns] = value[0]
                    out[c // 2, 1, inside, columns] = value[1]
                else:
                    summed[0, a, here, :] = value[0]
                    summed[1, a, here, :] = value[1]
        return carry

    lax.fori_loop(0, rows // sub, back, 0)
    if last:
        return

    def read(here, a):
        return summed[0, a, here, :], summed[1, a, here, :]

    def write(part, value):
        out[part] = value

    forward_y(read, write, spectrum, matrices, turns)


def weigh(level, first_level, place, freqs, ref_slow, tiles, weights):
    def full(value):
        return jnp.full((sub, inner), value, jnp.float32)

    lower, upper = full(ref_slow[level, 0]), full(ref_slow[level, 1])
    pace = depth_step * full(freqs[place[0]])
    inverse_gap = 1.0 / (upper - lower)
    turn = cis(pace * (lower - upper))

    z = 2 * place[0] + place[1]
    for n in range(ring):
        source = (z + n) % ring
        tile = tiles[n]

        def step(c, carry, source=source, tile=tile):
            from_y = c // 2
            here = pl.ds(pl.multiple_of(source // 2 * quarter + c % 2 * sub, sub), sub)
            for t in range(2):
                first = (2 * (level - first_level) + t) * quarter + c % 2 * sub
                slowness = 1.0 / tile[from_y, pl.ds(pl.multiple_of(first, sub), sub), :]
                excess = slowness - lower
                upper_weight = jnp.clip(excess * inverse_gap, 0.0, 1.0)
                lower_weight = 1.0 - upper_weight
                phase = cis(pace * excess)
                other = times(phase, turn)
                a = 2 * (source % 2 * 4 + from_y) + t
                weights[0, a, here, :] = lower_weight * phase[0]
                weights[1, a, here, :] = lower_weight * phase[1]
                weights[2, a, here, :] = upper_weight * other[0]
                weights[3, a, here, :] = upper_weight * other[1]
            return carry

        lax.fori_loop(0, 8, step, 0, unroll=2)


def propagators(level, place, freqs, ref_slow):
    lane = lax.broadcasted_iota(jnp.int32, (sub, inner), 1)
    sub_row = lax.broadcasted_iota(jnp.int32, (sub, inner), 0)
    fy = folded(place[2] // 2 + outer * (half * (place[2] % 2) + lane % half))
    fy = fy * fy
    squares = []
    for branch in range(2):
        wave = jnp.full((sub, inner), freqs[place[0]]) * jnp.full((sub, inner), ref_slow[level, branch])
        squares.append(wave * wave)

    def at(c, k):
        fx = folded(2 * k + jnp.where(lane < half, 0, 1) + outer * (c * sub + sub_row))
        square = fx * fx + fy
        shifts = []
        for branch in range(2):
            target = squares[branch] - square
            cycles = depth_step * jnp.sqrt(jnp.abs(target))
            cosine, sine = cis(cycles)
            live = target >= 0
            shifts.append(
                (
                    jnp.where(live, cosine, jnp.exp(-two_pi * cycles)),
                    jnp.where(live, sine, 0.0),
                )
            )
        return shifts

    return at


def propagator_kernel(place, freqs, ref_slow, *tables):
    for level, table in enumerate(tables):
        at = propagators(level, place, freqs, ref_slow)

        def step(c, carry, at=at, table=table):
            here = block_rows(c)
            second_half = pl.ds(pl.multiple_of(inner + c * sub, sub), sub)
            for k in range(outer // 2):
                columns = slice(k * inner, (k + 1) * inner)
                for branch, factor in enumerate(at(c, k)):
                    table[branch, here, columns] = factor[0]
                    table[branch, second_half, columns] = factor[1]
            return carry

        lax.fori_loop(0, inner // sub, step, 0)


def weigh_kernel(first_level, place, freqs, ref_slow, *refs):
    tiles = refs[:ring]
    for n, weights in enumerate(refs[ring:]):
        weigh(first_level + n, first_level, place, freqs, ref_slow, tiles, weights)


def slab_rows(a, top, c):
    return ((a // 4 * 2 + top) * 4 + a % 4) * rows + c * sub


def plane_chunk(a, top, c):
    return c // 2 * 8 + a % 4 * 2 + top, a // 4 * quarter + c % 2 * sub


def plane_rows(a, top, c):
    chunk, row = plane_chunk(a, top, c)
    return chunk * rows + row


def shift_kernel(
    rows_of,
    arrived,
    table,
    there_matrices,
    back_matrices,
    turns,
    out,
    spectrum,
    shifted,
    lane_turn,
):
    fill_lane_turns(lane_turn)
    lane = lax.broadcasted_iota(jnp.int32, (sub, inner), 1)
    low_lanes = lane < half
    groups = outer // 2
    steps = inner // sub

    def there(top, c, carry):
        position = top * half + c * sub
        here = pl.ds(pl.multiple_of(position, sub), sub)
        second_half = pl.ds(pl.multiple_of(inner + position, sub), sub)
        values = []
        for a in range(groups):
            first = arrived[pl.ds(pl.multiple_of(rows_of(a, top, c), sub), sub), :]
            second = arrived[pl.ds(pl.multiple_of(rows_of(a + groups, top, c), sub), sub), :]
            total, differ = first + second, first - second
            value = (
                jnp.where(low_lanes, total, pltpu.roll(differ, half, 1)),
                jnp.where(low_lanes, pltpu.roll(total, half, 1), differ),
            )
            turn = (lane_turn[0, a : a + 1, :], lane_turn[1, a : a + 1, :])
            values.append(value if a == 0 else times_conj(value, turn))
        values = dft(values, -1)
        for k in range(groups):
            value = times_conj(values[k], (turns[0, k, here, :], turns[1, k, here, :]))
            columns = slice(k * inner, (k + 1) * inner)
            spectrum[here, columns] = value[0]
            spectrum[second_half, columns] = value[1]
        return carry

    for top in range(2):
        lax.fori_loop(0, half // sub, functools.partial(there, top), 0, unroll=half // sub)
    matrix = (there_matrices[0], there_matrices[1])
    for n in range(4):
        columns = slice(n * 2 * inner, (n + 1) * 2 * inner)
        spectrum[:, columns] = mix(matrix, cut(spectrum[:, columns]))

    def propagate(c, carry):
        here = block_rows(c)
        second_half = pl.ds(pl.multiple_of(inner + c * sub, sub), sub)
        for k in range(groups):
            columns = slice(k * inner, (k + 1) * inner)
            value = (spectrum[here, columns], spectrum[second_half, columns])
            for branch in range(2):
                moved = times(value, (table[branch, here, columns], table[branch, second_half, columns]))
                shifted[branch, here, columns] = moved[0]
                shifted[branch, second_half, columns] = moved[1]
        return carry

    lax.fori_loop(0, steps, propagate, 0)
    matrix = (back_matrices[0], back_matrices[1])
    for branch in range(2):
        for n in range(4):
            columns = slice(n * 2 * inner, (n + 1) * 2 * inner)
            shifted[branch, :, columns] = mix(matrix, cut(shifted[branch, :, columns]))

    for top in range(2):

        def back(c, carry, top=top):
            position = top * half + c * sub
            here = pl.ds(pl.multiple_of(position, sub), sub)
            second_half = pl.ds(pl.multiple_of(inner + position, sub), sub)
            for branch in range(2):
                values = []
                for k in range(groups):
                    columns = slice(k * inner, (k + 1) * inner)
                    value = (shifted[branch, here, columns], shifted[branch, second_half, columns])
                    values.append(times(value, (turns[0, k, here, :], turns[1, k, here, :])))
                values = dft(values, 1)
                for a in range(groups):
                    value = values[a]
                    if a > 0:
                        value = times(value, (lane_turn[0, a : a + 1, :], lane_turn[1, a : a + 1, :]))
                    even = jnp.where(low_lanes, value[0], pltpu.roll(value[1], half, 1))
                    odd = jnp.where(low_lanes, pltpu.roll(value[0], half, 1), value[1])
                    for at, result in ((a, even + odd), (a + groups, even - odd)):
                        chunk, row = plane_chunk(at, top, c)
                        out[chunk, branch, pl.ds(pl.multiple_of(row, sub), sub), :] = result
            return carry

        lax.fori_loop(0, half // sub, back, 0, unroll=half // sub)


def call(kernel, shapes, scratch, scalars, operands):
    vmem = pl.BlockSpec(memory_space=pltpu.VMEM)
    smem = pl.BlockSpec(memory_space=pltpu.SMEM)
    return pl.pallas_call(
        kernel,
        out_shape=[jax.ShapeDtypeStruct(s, jnp.float32) for s in shapes],
        in_specs=[smem] * len(scalars) + [vmem] * len(operands),
        out_specs=[vmem] * len(shapes),
        scratch_shapes=[pltpu.VMEM(s, jnp.float32) for s in scratch],
        compiler_params=pltpu.CompilerParams(vmem_limit_bytes=12 * 1024 * 1024),
    )(*scalars, *operands)


def exchange(values, axes):
    return lax.all_to_all(values, axes, split_axis=0, concat_axis=0, tiled=True)


def around_z(tiles, first, last):
    axes = ("zl", "zh")
    index = [n % 2 * 4 + n // 2 for n in range(ring)]
    down = [(index[n], index[n - 1]) for n in range(ring)]
    up = [(index[n - 1], index[n]) for n in range(ring)]
    tiles = dict(tiles)
    for n in range(first, last):
        tiles[n] = lax.ppermute(tiles[n - 1], axes, down)
        if n < ring // 2:
            tiles[ring - n] = lax.ppermute(tiles[(ring + 1 - n) % ring], axes, up)
    return tiles


def shards(wavefield, freqs, velocity, ref_slow):
    zh, zl = lax.axis_index("zh"), lax.axis_index("zl")
    part = (lax.axis_index("y") * 4 + lax.axis_index("x")) * 2 + lax.axis_index("c")
    place = jnp.stack([zh, zl, part])

    fy_matrix = np.stack(forward_y_matrix())
    iy_matrix = np.stack(inverse_y_matrix())
    fx_matrix = np.stack(x_matrix(-1))
    ix_matrix = np.stack(x_matrix(1))
    turn_x = np.stack(x_turns())

    plane = ("y", "x", "c")
    packed = (parts, rows, inner)
    spectrum_shape = (outer, rows, 2 * inner)
    y_turns_shape = (2, outer, inner)
    folded_shape = (2 * inner, length // 2)

    (sent,) = call(
        start_kernel,
        [(4, message, inner)],
        [spectrum_shape, y_turns_shape],
        (freqs,),
        (wavefield, velocity, fy_matrix),
    )
    sent = exchange(sent, ("y",))
    sent, cells = lax.optimization_barrier((sent[:, :cell_start], sent[:, cell_start:]))
    common = (place, cells[:, -1, 0], ref_slow)
    first_tile = cells[:, :level_rows]
    later_tile = cells[:, level_rows : depth * level_rows]
    arrived = exchange(sent.reshape(packed), ("zh", "c", "x"))
    tables = call(propagator_kernel, [(2, *folded_shape)] * depth, [], common, ())
    weights = []
    for level in range(depth):
        if level == 0:
            arrived, first_tile, later_tile = lax.optimization_barrier(
                (arrived, first_tile, later_tile)
            )
            tiles = around_z({0: first_tile}, 1, 5)
        elif level == 1:
            sent, later_tile = lax.optimization_barrier((sent, later_tile))
            tiles = around_z({0: later_tile}, 1, 3)
            arrived, tiles = lax.optimization_barrier((exchange(sent, plane), tiles))
            tiles = around_z(tiles, 3, 5)
        else:
            arrived = exchange(sent, plane)
        if level < 2:
            weights += call(
                functools.partial(weigh_kernel, level),
                [(4, outer, rows, inner)] * (depth - 1 if level else 1),
                [],
                common,
                [tiles[n] for n in range(ring)],
            )
        (shifted,) = call(
            functools.partial(shift_kernel, plane_rows if level else slab_rows),
            [(parts, 2, rows, inner)],
            [folded_shape, (2, *folded_shape), (2, outer // 2, inner)],
            (),
            (arrived.reshape(length, inner), tables[level], fx_matrix, ix_matrix, turn_x),
        )
        moved = exchange(shifted, plane)
        last = level == depth - 1
        (sent,) = call(
            functools.partial(combine_kernel, last),
            [(4, 2, quarter, length) if last else packed],
            [(2, *spectrum_shape), (2, outer, rows, inner), spectrum_shape, y_turns_shape],
            (),
            (moved, weights[level], iy_matrix, fy_matrix),
        )
    back = exchange(exchange(sent, ("zh",)), ("y",))
    return back.transpose(1, 0, 2, 3).reshape(2, 1, rows, length)


def solution(mesh):
    axes = ("zl", "y", "zh", "x", "c")
    return jax.shard_map(
        shards,
        mesh=Mesh(mesh.devices.reshape(2, 4, 4, 4, 2), axes),
        in_specs=(
            P(None, axes[:2], axes[2:], None),
            P(axes[:2]),
            P(None, axes[2:], axes[:2]),
            P(),
        ),
        out_specs=P(None, axes[:2], axes[2:], None),
        check_vma=False,
    )
```

```python
import functools
import math

import jax
import jax.numpy as jnp
import numpy as np
from jax import lax
from jax.experimental import pallas as pl
from jax.experimental.pallas import tpu as pltpu
from jax.sharding import Mesh
from jax.sharding import PartitionSpec as P

two_pi = 2.0 * math.pi
depth_step = 2.0

length = 2048
outer = 16
inner = 128
half = 64
rows = 64
parts = 32
sub = 8
depth = 3
ring = 8
quarter = 16
level_rows = 2 * quarter
cell_start = 8 * rows
freq_start = cell_start + depth * level_rows
message = freq_start + sub


def split_bf16(matrix):
    matrix = np.asarray(matrix, np.float32)
    high = matrix.astype(jnp.bfloat16)
    low = (matrix - high.astype(np.float32)).astype(jnp.bfloat16)
    return high, low


def dft_inner(sign):
    index = np.arange(inner)
    angle = sign * two_pi / inner * (index[:, None] * index[None, :] % inner)
    scale = 1.0 / math.sqrt(length)
    return np.cos(angle) * scale, np.sin(angle) * scale


def packed_order():
    low = np.arange(half)
    return np.concatenate([low, inner + low, half + low, inner + half + low])


def forward_y_matrix():
    real, imag = dft_inner(-1)
    full = np.block([[real, imag], [-imag, real]])
    return split_bf16(full[:, packed_order()])


def inverse_y_matrix():
    real, imag = dft_inner(1)
    full = np.block([[real, imag], [-imag, real]])
    return split_bf16(full[packed_order(), :])


def x_matrix(sign):
    real, imag = dft_inner(sign)
    return split_bf16(np.block([[real, -imag], [imag, real]]))


def x_turns():
    upper = (np.arange(inner) >= half).astype(np.int64)
    k = 2 * np.arange(outer // 2)[:, None, None] + upper[None, None, :]
    angle = two_pi / length * (k * np.arange(inner)[None, :, None])
    return np.cos(angle).astype(np.float32), np.sin(angle).astype(np.float32)


def fit_even(function, terms):
    nodes = np.cos(np.pi * (np.arange(256) + 0.5) / 256)
    basis = np.stack([nodes ** (2 * n) for n in range(terms)], axis=1)
    solved = np.linalg.lstsq(basis, function(nodes), rcond=None)[0]
    return [float(c) for c in solved]


cos_fit = fit_even(lambda z: np.cos(np.pi * z), 9)
sin_fit = fit_even(lambda z: np.pi * np.sinc(z), 9)


def cis(cycles):
    z = 2.0 * (cycles - jnp.floor(cycles + 0.5))
    square = z * z
    cosine = cos_fit[-1]
    for c in cos_fit[-2::-1]:
        cosine = cosine * square + c
    sine = sin_fit[-1]
    for c in sin_fit[-2::-1]:
        sine = sine * square + c
    return cosine, sine * z


def fill_y_turns(turns):
    k = lax.broadcasted_iota(jnp.int32, (outer, inner), 0)
    b = lax.broadcasted_iota(jnp.int32, (outer, inner), 1)
    turns[0], turns[1] = cis((k * b).astype(jnp.float32) * (1.0 / length))


def fill_lane_turns(turns):
    a = lax.broadcasted_iota(jnp.int32, (outer // 2, inner), 0)
    lane = lax.broadcasted_iota(jnp.int32, (outer // 2, inner), 1)
    turns[0], turns[1] = cis(jnp.where(lane < half, 0, a).astype(jnp.float32) * (1.0 / outer))


def times(a, b):
    return (a[0] * b[0] - a[1] * b[1], a[0] * b[1] + a[1] * b[0])


def times_conj(a, b):
    return (a[0] * b[0] + a[1] * b[1], a[1] * b[0] - a[0] * b[1])


def plus(a, b):
    return (a[0] + b[0], a[1] + b[1])


def minus(a, b):
    return (a[0] - b[0], a[1] - b[1])


def times_root(a, power, n, sign):
    eighth = (8 * power) % (8 * n)
    real, imag = a
    if eighth % n == 0:
        step = (eighth // n) % 8
        if sign < 0:
            step = (8 - step) % 8
        if step == 0:
            return a
        if step == 2:
            return (-imag, real)
        if step == 4:
            return (-real, -imag)
        if step == 6:
            return (imag, -real)
        root = math.sqrt(0.5)
        total = (real + imag) * root
        differ = (real - imag) * root
        if step == 1:
            return (differ, total)
        if step == 3:
            return (-total, differ)
        if step == 5:
            return (-differ, -total)
        return (total, -differ)
    angle = sign * two_pi * power / n
    c, s = math.cos(angle), math.sin(angle)
    return (real * c - imag * s, real * s + imag * c)


def dft(values, sign):
    n = len(values)
    if n == 2:
        return [plus(*values), minus(*values)]
    if n == 4:
        t0, t1 = plus(values[0], values[2]), minus(values[0], values[2])
        t2, t3 = plus(values[1], values[3]), minus(values[1], values[3])
        if sign > 0:
            y1 = (t1[0] - t3[1], t1[1] + t3[0])
            y3 = (t1[0] + t3[1], t1[1] - t3[0])
        else:
            y1 = (t1[0] + t3[1], t1[1] - t3[0])
            y3 = (t1[0] - t3[1], t1[1] + t3[0])
        return [plus(t0, t2), y1, minus(t0, t2), y3]
    radix = 2 if n == 8 else 4
    m = n // radix
    inside = [dft(values[s::radix], sign) for s in range(radix)]
    out = [None] * n
    for k in range(m):
        turned = [times_root(inside[s][k], s * k, n, sign) for s in range(radix)]
        for step, value in enumerate(dft(turned, sign)):
            out[k + m * step] = value
    return out


def cut(x):
    high = x.astype(jnp.bfloat16)
    low = (x - high.astype(jnp.float32)).astype(jnp.bfloat16)
    return high, low


def product(a, b):
    return jnp.dot(a, b, preferred_element_type=jnp.float32)


def mix(a, b):
    (a_high, a_low), (b_high, b_low) = a, b
    left = jnp.concatenate([a_high, a_high, a_low], axis=1)
    right = jnp.concatenate([b_high, b_low, b_high], axis=0)
    return product(left, right)


def folded(number):
    return jnp.minimum(number, length - number).astype(jnp.float32) * (1.0 / length)


def block_rows(step):
    return pl.ds(pl.multiple_of(step * sub, sub), sub)


def forward_y(read, write, spectrum, matrices, turns):
    turn_cos, turn_sin = turns[0], turns[1]

    def step(c, carry):
        here = block_rows(c)
        values = dft([read(here, a) for a in range(outer)], -1)
        for k in range(outer):
            turn = (turn_cos[k : k + 1, :], turn_sin[k : k + 1, :])
            value = values[k] if k == 0 else times_conj(values[k], turn)
            spectrum[k, here, :inner] = value[0]
            spectrum[k, here, inner:] = value[1]
        return carry

    lax.fori_loop(0, rows // sub, step, 0)
    matrix = (matrices[0], matrices[1])
    for k in range(0, outer, 4):
        block = spectrum[k : k + 4].reshape(4 * rows, 2 * inner)
        result = mix(cut(block), matrix)
        for n in range(4):
            one = result[n * rows : (n + 1) * rows]
            write(2 * (k + n), one[:, :inner])
            write(2 * (k + n) + 1, one[:, inner:])


def start_kernel(freqs, wavefield, velocity, matrices, out, spectrum, turns):
    fill_y_turns(turns)

    def read(here, a):
        columns = slice(a * inner, (a + 1) * inner)
        return wavefield[0, 0, here, columns], wavefield[1, 0, here, columns]

    def write(part, value):
        y, x, c = part // 8, part // 2 % 4, part % 2
        place = (4 * c + x) * rows
        out[y, place : place + rows, :] = value

    forward_y(read, write, spectrum, matrices, turns)
    for y in range(4):
        for level in range(depth):
            for t in range(2):
                place = cell_start + (2 * level + t) * quarter
                out[y, place : place + quarter, :] = velocity[
                    level, y * quarter : (y + 1) * quarter, t * inner : (t + 1) * inner
                ]
        out[y, freq_start:, :] = jnp.full((sub, inner), freqs[0], jnp.float32)


def combine_kernel(last, moved, weights, back_matrices, matrices, out, fields, *scratch):
    fields_kernel(moved, back_matrices, fields)
    sum_kernel(last, fields, weights, matrices, out, *scratch)


def fields_kernel(moved, back_matrices, fields):
    matrix = (back_matrices[0], back_matrices[1])
    for branch in range(2):
        for k in range(0, outer, 4):
            block = jnp.concatenate(
                [
                    jnp.concatenate([moved[2 * n, branch], moved[2 * n + 1, branch]], axis=1)
                    for n in range(k, k + 4)
                ],
                axis=0,
            )
            result = mix(cut(block), matrix)
            fields[branch, k : k + 4] = result.reshape(4, rows, 2 * inner)


def sum_kernel(last, fields, weights, matrices, out, summed, spectrum, turns):
    fill_y_turns(turns)
    turn_cos, turn_sin = turns[0], turns[1]

    def back(c, carry):
        here = block_rows(c)
        for branch in range(2):
            values = []
            for k in range(outer):
                value = (fields[branch, k, here, :inner], fields[branch, k, here, inner:])
                turn = (turn_cos[k : k + 1, :], turn_sin[k : k + 1, :])
                values.append(value if k == 0 else times(value, turn))
            values = dft(values, 1)
            for a in range(outer):
                weight = (weights[2 * branch, a, here, :], weights[2 * branch + 1, a, here, :])
                value = times(values[a], weight)
                if branch == 1:
                    value = plus(value, (summed[0, a, here, :], summed[1, a, here, :]))
                if last and branch == 1:
                    columns = slice(a * inner, (a + 1) * inner)
                    inside = pl.ds(pl.multiple_of(c % 2 * sub, sub), sub)
                    out[c // 2, 0, inside, columns] = value[0]
                    out[c // 2, 1, inside, columns] = value[1]
                else:
                    summed[0, a, here, :] = value[0]
                    summed[1, a, here, :] = value[1]
        return carry

    lax.fori_loop(0, rows // sub, back, 0)
    if last:
        return

    def read(here, a):
        return summed[0, a, here, :], summed[1, a, here, :]

    def write(part, value):
        out[part] = value

    forward_y(read, write, spectrum, matrices, turns)


def weigh(level, first_level, place, freqs, ref_slow, tiles, weights):
    def full(value):
        return jnp.full((sub, inner), value, jnp.float32)

    lower, upper = full(ref_slow[level, 0]), full(ref_slow[level, 1])
    pace = depth_step * full(freqs[place[0]])
    inverse_gap = 1.0 / (upper - lower)
    turn = cis(pace * (lower - upper))

    z = 2 * place[0] + place[1]
    for n in range(ring):
        source = (z + n) % ring
        tile = tiles[n]

        def step(c, carry, source=source, tile=tile):
            from_y = c // 2
            here = pl.ds(pl.multiple_of(source // 2 * quarter + c % 2 * sub, sub), sub)
            for t in range(2):
                first = (2 * (level - first_level) + t) * quarter + c % 2 * sub
                slowness = 1.0 / tile[from_y, pl.ds(pl.multiple_of(first, sub), sub), :]
                excess = slowness - lower
                upper_weight = jnp.clip(excess * inverse_gap, 0.0, 1.0)
                lower_weight = 1.0 - upper_weight
                phase = cis(pace * excess)
                other = times(phase, turn)
                a = 2 * (source % 2 * 4 + from_y) + t
                weights[0, a, here, :] = lower_weight * phase[0]
                weights[1, a, here, :] = lower_weight * phase[1]
                weights[2, a, here, :] = upper_weight * other[0]
                weights[3, a, here, :] = upper_weight * other[1]
            return carry

        lax.fori_loop(0, 8, step, 0, unroll=2)


def propagators(level, place, freqs, ref_slow):
    lane = lax.broadcasted_iota(jnp.int32, (sub, inner), 1)
    sub_row = lax.broadcasted_iota(jnp.int32, (sub, inner), 0)
    fy = folded(place[2] // 2 + outer * (half * (place[2] % 2) + lane % half))
    fy = fy * fy
    squares = []
    for branch in range(2):
        wave = jnp.full((sub, inner), freqs[place[0]]) * jnp.full((sub, inner), ref_slow[level, branch])
        squares.append(wave * wave)

    def at(c, k):
        fx = folded(2 * k + jnp.where(lane < half, 0, 1) + outer * (c * sub + sub_row))
        square = fx * fx + fy
        shifts = []
        for branch in range(2):
            target = squares[branch] - square
            cycles = depth_step * jnp.sqrt(jnp.abs(target))
            cosine, sine = cis(cycles)
            live = target >= 0
            shifts.append(
                (
                    jnp.where(live, cosine, jnp.exp(-two_pi * cycles)),
                    jnp.where(live, sine, 0.0),
                )
            )
        return shifts

    return at


def propagator_kernel(place, freqs, ref_slow, *tables):
    for level, table in enumerate(tables):
        at = propagators(level, place, freqs, ref_slow)

        def step(c, carry, at=at, table=table):
            here = block_rows(c)
            second_half = pl.ds(pl.multiple_of(inner + c * sub, sub), sub)
            for k in range(outer // 2):
                columns = slice(k * inner, (k + 1) * inner)
                for branch, factor in enumerate(at(c, k)):
                    table[branch, here, columns] = factor[0]
                    table[branch, second_half, columns] = factor[1]
            return carry

        lax.fori_loop(0, inner // sub, step, 0)


def weigh_kernel(first_level, place, freqs, ref_slow, *refs):
    tiles = refs[:ring]
    for n, weights in enumerate(refs[ring:]):
        weigh(first_level + n, first_level, place, freqs, ref_slow, tiles, weights)


def slab_rows(a, top, c):
    return ((a // 4 * 2 + top) * 4 + a % 4) * rows + c * sub


def plane_chunk(a, top, c):
    return c // 2 * 8 + a % 4 * 2 + top, a // 4 * quarter + c % 2 * sub


def plane_rows(a, top, c):
    chunk, row = plane_chunk(a, top, c)
    return chunk * rows + row


def shift_kernel(rows_of, arrived, table, there_matrices, back_matrices, turns, out, spectrum, *scratch):
    forward_x_kernel(rows_of, arrived, there_matrices, turns, spectrum, scratch[1])
    back_x_kernel(spectrum, table, back_matrices, turns, out, *scratch)


def forward_x_kernel(rows_of, arrived, there_matrices, turns, spectrum, lane_turn):
    fill_lane_turns(lane_turn)
    lane = lax.broadcasted_iota(jnp.int32, (sub, inner), 1)
    low_lanes = lane < half
    groups = outer // 2
    steps = inner // sub

    def there(top, c, carry):
        position = top * half + c * sub
        here = pl.ds(pl.multiple_of(position, sub), sub)
        second_half = pl.ds(pl.multiple_of(inner + position, sub), sub)
        values = []
        for a in range(groups):
            first = arrived[pl.ds(pl.multiple_of(rows_of(a, top, c), sub), sub), :]
            second = arrived[pl.ds(pl.multiple_of(rows_of(a + groups, top, c), sub), sub), :]
            total, differ = first + second, first - second
            value = (
                jnp.where(low_lanes, total, pltpu.roll(differ, half, 1)),
                jnp.where(low_lanes, pltpu.roll(total, half, 1), differ),
            )
            turn = (lane_turn[0, a : a + 1, :], lane_turn[1, a : a + 1, :])
            values.append(value if a == 0 else times_conj(value, turn))
        values = dft(values, -1)
        for k in range(groups):
            value = times_conj(values[k], (turns[0, k, here, :], turns[1, k, here, :]))
            columns = slice(k * inner, (k + 1) * inner)
            spectrum[here, columns] = value[0]
            spectrum[second_half, columns] = value[1]
        return carry

    for top in range(2):
        lax.fori_loop(0, half // sub, functools.partial(there, top), 0, unroll=half // sub)
    matrix = (there_matrices[0], there_matrices[1])
    for n in range(4):
        columns = slice(n * 2 * inner, (n + 1) * 2 * inner)
        spectrum[:, columns] = mix(matrix, cut(spectrum[:, columns]))


def back_x_kernel(spectrum, table, back_matrices, turns, out, shifted, lane_turn):
    fill_lane_turns(lane_turn)
    lane = lax.broadcasted_iota(jnp.int32, (sub, inner), 1)
    low_lanes = lane < half
    groups = outer // 2
    steps = inner // sub

    def propagate(c, carry):
        here = block_rows(c)
        second_half = pl.ds(pl.multiple_of(inner + c * sub, sub), sub)
        for k in range(groups):
            columns = slice(k * inner, (k + 1) * inner)
            value = (spectrum[here, columns], spectrum[second_half, columns])
            for branch in range(2):
                moved = times(value, (table[branch, here, columns], table[branch, second_half, columns]))
                shifted[branch, here, columns] = moved[0]
                shifted[branch, second_half, columns] = moved[1]
        return carry

    lax.fori_loop(0, steps, propagate, 0)
    matrix = (back_matrices[0], back_matrices[1])
    for branch in range(2):
        for n in range(4):
            columns = slice(n * 2 * inner, (n + 1) * 2 * inner)
            shifted[branch, :, columns] = mix(matrix, cut(shifted[branch, :, columns]))

    for top in range(2):

        def back(c, carry, top=top):
            position = top * half + c * sub
            here = pl.ds(pl.multiple_of(position, sub), sub)
            second_half = pl.ds(pl.multiple_of(inner + position, sub), sub)
            for branch in range(2):
                values = []
                for k in range(groups):
                    columns = slice(k * inner, (k + 1) * inner)
                    value = (shifted[branch, here, columns], shifted[branch, second_half, columns])
                    values.append(times(value, (turns[0, k, here, :], turns[1, k, here, :])))
                values = dft(values, 1)
                for a in range(groups):
                    value = values[a]
                    if a > 0:
                        value = times(value, (lane_turn[0, a : a + 1, :], lane_turn[1, a : a + 1, :]))
                    even = jnp.where(low_lanes, value[0], pltpu.roll(value[1], half, 1))
                    odd = jnp.where(low_lanes, pltpu.roll(value[0], half, 1), value[1])
                    for at, result in ((a, even + odd), (a + groups, even - odd)):
                        chunk, row = plane_chunk(at, top, c)
                        out[chunk, branch, pl.ds(pl.multiple_of(row, sub), sub), :] = result
            return carry

        lax.fori_loop(0, half // sub, back, 0, unroll=half // sub)


def call(kernel, shapes, scratch, scalars, operands):
    vmem = pl.BlockSpec(memory_space=pltpu.VMEM)
    smem = pl.BlockSpec(memory_space=pltpu.SMEM)
    return pl.pallas_call(
        kernel,
        out_shape=[jax.ShapeDtypeStruct(s, jnp.float32) for s in shapes],
        in_specs=[smem] * len(scalars) + [vmem] * len(operands),
        out_specs=[vmem] * len(shapes),
        scratch_shapes=[pltpu.VMEM(s, jnp.float32) for s in scratch],
        compiler_params=pltpu.CompilerParams(vmem_limit_bytes=12 * 1024 * 1024),
    )(*scalars, *operands)


def exchange(values, axes):
    return lax.all_to_all(values, axes, split_axis=0, concat_axis=0, tiled=True)


def around_z(tiles, first, last):
    axes = ("zl", "zh")
    index = [n % 2 * 4 + n // 2 for n in range(ring)]
    down = [(index[n], index[n - 1]) for n in range(ring)]
    up = [(index[n - 1], index[n]) for n in range(ring)]
    tiles = dict(tiles)
    for n in range(first, last):
        tiles[n] = lax.ppermute(tiles[n - 1], axes, down)
        if n < ring // 2:
            tiles[ring - n] = lax.ppermute(tiles[(ring + 1 - n) % ring], axes, up)
    return tiles


def shards(wavefield, freqs, velocity, ref_slow):
    zh, zl = lax.axis_index("zh"), lax.axis_index("zl")
    part = (lax.axis_index("y") * 4 + lax.axis_index("x")) * 2 + lax.axis_index("c")
    place = jnp.stack([zh, zl, part])

    fy_matrix = np.stack(forward_y_matrix())
    iy_matrix = np.stack(inverse_y_matrix())
    fx_matrix = np.stack(x_matrix(-1))
    ix_matrix = np.stack(x_matrix(1))
    turn_x = np.stack(x_turns())

    plane = ("y", "x", "c")
    packed = (parts, rows, inner)
    spectrum_shape = (outer, rows, 2 * inner)
    y_turns_shape = (2, outer, inner)
    folded_shape = (2 * inner, length // 2)

    (sent,) = call(
        start_kernel,
        [(4, message, inner)],
        [spectrum_shape, y_turns_shape],
        (freqs,),
        (wavefield, velocity, fy_matrix),
    )
    sent = exchange(sent, ("y",))
    sent, cells = lax.optimization_barrier((sent[:, :cell_start], sent[:, cell_start:]))
    common = (place, cells[:, -1, 0], ref_slow)
    first_tile = cells[:, :level_rows]
    later_tile = cells[:, level_rows : depth * level_rows]
    arrived = exchange(sent.reshape(packed), ("zh", "c", "x"))
    tables = call(propagator_kernel, [(2, *folded_shape)] * depth, [], common, ())
    weights = []
    for level in range(depth):
        if level == 0:
            arrived, first_tile, later_tile = lax.optimization_barrier(
                (arrived, first_tile, later_tile)
            )
            tiles = around_z({0: first_tile}, 1, 5)
        elif level == 1:
            sent, later_tile = lax.optimization_barrier((sent, later_tile))
            tiles = around_z({0: later_tile}, 1, 3)
            arrived, tiles = lax.optimization_barrier((exchange(sent, plane), tiles))
            tiles = around_z(tiles, 3, 5)
        else:
            arrived = exchange(sent, plane)
        if level < 2:
            weights += call(
                functools.partial(weigh_kernel, level),
                [(4, outer, rows, inner)] * (depth - 1 if level else 1),
                [],
                common,
                [tiles[n] for n in range(ring)],
            )
        last = level == depth - 1
        read = plane_rows if level else slab_rows
        arrived = arrived.reshape(length, inner)
        x_scratch = [(2, *folded_shape), (2, outer // 2, inner)]
        y_scratch = [(2, outer, rows, inner), spectrum_shape, y_turns_shape]
        if last:
            (shifted,) = call(
                functools.partial(shift_kernel, read),
                [(parts, 2, rows, inner)],
                [folded_shape, *x_scratch],
                (),
                (arrived, tables[level], fx_matrix, ix_matrix, turn_x),
            )
            moved = exchange(shifted, plane)
            (sent,) = call(
                functools.partial(combine_kernel, last),
                [(4, 2, quarter, length)],
                [(2, *spectrum_shape), *y_scratch],
                (),
                (moved, weights[level], iy_matrix, fy_matrix),
            )
        else:
            (spectrum,) = call(
                functools.partial(forward_x_kernel, read),
                [folded_shape],
                x_scratch[1:],
                (),
                (arrived, fx_matrix, turn_x),
            )
            (shifted,) = call(
                back_x_kernel,
                [(parts, 2, rows, inner)],
                x_scratch,
                (),
                (spectrum, tables[level], ix_matrix, turn_x),
            )
            moved = exchange(shifted, plane)
            (fields,) = call(fields_kernel, [(2, *spectrum_shape)], [], (), (moved, iy_matrix))
            (sent,) = call(
                functools.partial(sum_kernel, last),
                [packed],
                y_scratch,
                (),
                (fields, weights[level], fy_matrix),
            )
    back = exchange(exchange(sent, ("zh",)), ("y",))
    return back.transpose(1, 0, 2, 3).reshape(2, 1, rows, length)


def solution(mesh):
    axes = ("zl", "y", "zh", "x", "c")
    return jax.shard_map(
        shards,
        mesh=Mesh(mesh.devices.reshape(2, 4, 4, 4, 2), axes),
        in_specs=(
            P(None, axes[:2], axes[2:], None),
            P(axes[:2]),
            P(None, axes[2:], axes[:2]),
            P(),
        ),
        out_specs=P(None, axes[:2], axes[2:], None),
        check_vma=False,
    )
```

```python
import functools
import math

import jax
import jax.numpy as jnp
import numpy as np
from jax import lax
from jax.experimental import pallas as pl
from jax.experimental.pallas import tpu as pltpu
from jax.sharding import Mesh
from jax.sharding import PartitionSpec as P

two_pi = 2.0 * math.pi
depth_step = 2.0

length = 2048
outer = 16
inner = 128
half = 64
rows = 64
parts = 32
sub = 8
depth = 3
ring = 8
quarter = 16
level_rows = 2 * quarter
cell_start = 8 * rows
freq_start = cell_start + depth * level_rows
message = freq_start + sub


def split_bf16(matrix):
    matrix = np.asarray(matrix, np.float32)
    high = matrix.astype(jnp.bfloat16)
    low = (matrix - high.astype(np.float32)).astype(jnp.bfloat16)
    return high, low


def dft_inner(sign):
    index = np.arange(inner)
    angle = sign * two_pi / inner * (index[:, None] * index[None, :] % inner)
    scale = 1.0 / math.sqrt(length)
    return np.cos(angle) * scale, np.sin(angle) * scale


def packed_order():
    low = np.arange(half)
    return np.concatenate([low, inner + low, half + low, inner + half + low])


def forward_y_matrix():
    real, imag = dft_inner(-1)
    full = np.block([[real, imag], [-imag, real]])
    return split_bf16(full[:, packed_order()])


def inverse_y_matrix():
    real, imag = dft_inner(1)
    full = np.block([[real, imag], [-imag, real]])
    return split_bf16(full[packed_order(), :])


def x_matrix(sign):
    real, imag = dft_inner(sign)
    return split_bf16(np.block([[real, -imag], [imag, real]]))


def x_turns():
    upper = (np.arange(inner) >= half).astype(np.int64)
    k = 2 * np.arange(outer // 2)[:, None, None] + upper[None, None, :]
    angle = two_pi / length * (k * np.arange(inner)[None, :, None])
    return np.cos(angle).astype(np.float32), np.sin(angle).astype(np.float32)


def fit_even(function, terms):
    nodes = np.cos(np.pi * (np.arange(256) + 0.5) / 256)
    basis = np.stack([nodes ** (2 * n) for n in range(terms)], axis=1)
    solved = np.linalg.lstsq(basis, function(nodes), rcond=None)[0]
    return [float(c) for c in solved]


cos_fit = fit_even(lambda z: np.cos(np.pi * z), 9)
sin_fit = fit_even(lambda z: np.pi * np.sinc(z), 9)


def cis(cycles):
    z = 2.0 * (cycles - jnp.floor(cycles + 0.5))
    square = z * z
    cosine = cos_fit[-1]
    for c in cos_fit[-2::-1]:
        cosine = cosine * square + c
    sine = sin_fit[-1]
    for c in sin_fit[-2::-1]:
        sine = sine * square + c
    return cosine, sine * z


def fill_y_turns(turns):
    k = lax.broadcasted_iota(jnp.int32, (outer, inner), 0)
    b = lax.broadcasted_iota(jnp.int32, (outer, inner), 1)
    turns[0], turns[1] = cis((k * b).astype(jnp.float32) * (1.0 / length))


def fill_lane_turns(turns):
    a = lax.broadcasted_iota(jnp.int32, (outer // 2, inner), 0)
    lane = lax.broadcasted_iota(jnp.int32, (outer // 2, inner), 1)
    turns[0], turns[1] = cis(jnp.where(lane < half, 0, a).astype(jnp.float32) * (1.0 / outer))


def times(a, b):
    return (a[0] * b[0] - a[1] * b[1], a[0] * b[1] + a[1] * b[0])


def times_conj(a, b):
    return (a[0] * b[0] + a[1] * b[1], a[1] * b[0] - a[0] * b[1])


def plus(a, b):
    return (a[0] + b[0], a[1] + b[1])


def minus(a, b):
    return (a[0] - b[0], a[1] - b[1])


def times_root(a, power, n, sign):
    eighth = (8 * power) % (8 * n)
    real, imag = a
    if eighth % n == 0:
        step = (eighth // n) % 8
        if sign < 0:
            step = (8 - step) % 8
        if step == 0:
            return a
        if step == 2:
            return (-imag, real)
        if step == 4:
            return (-real, -imag)
        if step == 6:
            return (imag, -real)
        root = math.sqrt(0.5)
        total = (real + imag) * root
        differ = (real - imag) * root
        if step == 1:
            return (differ, total)
        if step == 3:
            return (-total, differ)
        if step == 5:
            return (-differ, -total)
        return (total, -differ)
    angle = sign * two_pi * power / n
    c, s = math.cos(angle), math.sin(angle)
    return (real * c - imag * s, real * s + imag * c)


def dft(values, sign):
    n = len(values)
    if n == 2:
        return [plus(*values), minus(*values)]
    if n == 4:
        t0, t1 = plus(values[0], values[2]), minus(values[0], values[2])
        t2, t3 = plus(values[1], values[3]), minus(values[1], values[3])
        if sign > 0:
            y1 = (t1[0] - t3[1], t1[1] + t3[0])
            y3 = (t1[0] + t3[1], t1[1] - t3[0])
        else:
            y1 = (t1[0] + t3[1], t1[1] - t3[0])
            y3 = (t1[0] - t3[1], t1[1] + t3[0])
        return [plus(t0, t2), y1, minus(t0, t2), y3]
    radix = 2 if n == 8 else 4
    m = n // radix
    inside = [dft(values[s::radix], sign) for s in range(radix)]
    out = [None] * n
    for k in range(m):
        turned = [times_root(inside[s][k], s * k, n, sign) for s in range(radix)]
        for step, value in enumerate(dft(turned, sign)):
            out[k + m * step] = value
    return out


def cut(x):
    high = x.astype(jnp.bfloat16)
    low = (x - high.astype(jnp.float32)).astype(jnp.bfloat16)
    return high, low


def product(a, b):
    return jnp.dot(a, b, preferred_element_type=jnp.float32)


def mix(a, b):
    (a_high, a_low), (b_high, b_low) = a, b
    left = jnp.concatenate([a_high, a_high, a_low], axis=1)
    right = jnp.concatenate([b_high, b_low, b_high], axis=0)
    return product(left, right)


def folded(number):
    return jnp.minimum(number, length - number).astype(jnp.float32) * (1.0 / length)


def block_rows(step):
    return pl.ds(pl.multiple_of(step * sub, sub), sub)


def forward_y(read, write, spectrum, matrices, turns):
    turn_cos, turn_sin = turns[0], turns[1]

    def step(c, carry):
        here = block_rows(c)
        values = dft([read(here, a) for a in range(outer)], -1)
        for k in range(outer):
            turn = (turn_cos[k : k + 1, :], turn_sin[k : k + 1, :])
            value = values[k] if k == 0 else times_conj(values[k], turn)
            spectrum[k, here, :inner] = value[0]
            spectrum[k, here, inner:] = value[1]
        return carry

    lax.fori_loop(0, rows // sub, step, 0)
    matrix = (matrices[0], matrices[1])
    for k in range(0, outer, 4):
        block = spectrum[k : k + 4].reshape(4 * rows, 2 * inner)
        result = mix(cut(block), matrix)
        for n in range(4):
            one = result[n * rows : (n + 1) * rows]
            write(2 * (k + n), one[:, :inner])
            write(2 * (k + n) + 1, one[:, inner:])


def start_kernel(freqs, wavefield, velocity, matrices, out, spectrum, turns):
    fill_y_turns(turns)

    def read(here, a):
        columns = slice(a * inner, (a + 1) * inner)
        return wavefield[0, 0, here, columns], wavefield[1, 0, here, columns]

    def write(part, value):
        y, x, c = part // 8, part // 2 % 4, part % 2
        place = (4 * c + x) * rows
        out[y, place : place + rows, :] = value

    forward_y(read, write, spectrum, matrices, turns)
    for y in range(4):
        for level in range(depth):
            for t in range(2):
                place = cell_start + (2 * level + t) * quarter
                out[y, place : place + quarter, :] = velocity[
                    level, y * quarter : (y + 1) * quarter, t * inner : (t + 1) * inner
                ]
        out[y, freq_start:, :] = jnp.full((sub, inner), freqs[0], jnp.float32)


def combine_kernel(last, moved, weights, back_matrices, matrices, out, fields, *scratch):
    fields_kernel(moved, back_matrices, fields)
    sum_kernel(last, fields, weights, matrices, out, *scratch)


def fields_kernel(moved, back_matrices, fields):
    matrix = (back_matrices[0], back_matrices[1])
    for branch in range(2):
        for k in range(0, outer, 4):
            block = jnp.concatenate(
                [
                    jnp.concatenate([moved[2 * n, branch], moved[2 * n + 1, branch]], axis=1)
                    for n in range(k, k + 4)
                ],
                axis=0,
            )
            result = mix(cut(block), matrix)
            fields[branch, k : k + 4] = result.reshape(4, rows, 2 * inner)


def sum_kernel(last, fields, weights, matrices, out, summed, spectrum, turns):
    fill_y_turns(turns)
    turn_cos, turn_sin = turns[0], turns[1]

    def back(c, carry):
        here = block_rows(c)
        for branch in range(2):
            values = []
            for k in range(outer):
                value = (fields[branch, k, here, :inner], fields[branch, k, here, inner:])
                turn = (turn_cos[k : k + 1, :], turn_sin[k : k + 1, :])
                values.append(value if k == 0 else times(value, turn))
            values = dft(values, 1)
            for a in range(outer):
                weight = (weights[2 * branch, a, here, :], weights[2 * branch + 1, a, here, :])
                value = times(values[a], weight)
                if branch == 1:
                    value = plus(value, (summed[0, a, here, :], summed[1, a, here, :]))
                if last and branch == 1:
                    columns = slice(a * inner, (a + 1) * inner)
                    inside = pl.ds(pl.multiple_of(c % 2 * sub, sub), sub)
                    out[c // 2, 0, inside, columns] = value[0]
                    out[c // 2, 1, inside, columns] = value[1]
                else:
                    summed[0, a, here, :] = value[0]
                    summed[1, a, here, :] = value[1]
        return carry

    lax.fori_loop(0, rows // sub, back, 0)
    if last:
        return

    def read(here, a):
        return summed[0, a, here, :], summed[1, a, here, :]

    def write(part, value):
        out[part] = value

    forward_y(read, write, spectrum, matrices, turns)


def weigh(level, first_level, place, freqs, ref_slow, tiles, weights):
    def full(value):
        return jnp.full((sub, inner), value, jnp.float32)

    lower, upper = full(ref_slow[level, 0]), full(ref_slow[level, 1])
    pace = depth_step * full(freqs[place[0]])
    inverse_gap = 1.0 / (upper - lower)
    turn = cis(pace * (lower - upper))

    z = 2 * place[0] + place[1]
    for n in range(ring):
        source = (z + n) % ring
        tile = tiles[n]

        def step(c, carry, source=source, tile=tile):
            from_y = c // 2
            here = pl.ds(pl.multiple_of(source // 2 * quarter + c % 2 * sub, sub), sub)
            for t in range(2):
                first = (2 * (level - first_level) + t) * quarter + c % 2 * sub
                slowness = 1.0 / tile[from_y, pl.ds(pl.multiple_of(first, sub), sub), :]
                excess = slowness - lower
                upper_weight = jnp.clip(excess * inverse_gap, 0.0, 1.0)
                lower_weight = 1.0 - upper_weight
                phase = cis(pace * excess)
                other = times(phase, turn)
                a = 2 * (source % 2 * 4 + from_y) + t
                weights[0, a, here, :] = lower_weight * phase[0]
                weights[1, a, here, :] = lower_weight * phase[1]
                weights[2, a, here, :] = upper_weight * other[0]
                weights[3, a, here, :] = upper_weight * other[1]
            return carry

        lax.fori_loop(0, 8, step, 0, unroll=2)


def propagators(level, place, freqs, ref_slow):
    lane = lax.broadcasted_iota(jnp.int32, (sub, inner), 1)
    sub_row = lax.broadcasted_iota(jnp.int32, (sub, inner), 0)
    fy = folded(place[2] // 2 + outer * (half * (place[2] % 2) + lane % half))
    fy = fy * fy
    squares = []
    for branch in range(2):
        wave = jnp.full((sub, inner), freqs[place[0]]) * jnp.full((sub, inner), ref_slow[level, branch])
        squares.append(wave * wave)

    def at(c, k):
        fx = folded(2 * k + jnp.where(lane < half, 0, 1) + outer * (c * sub + sub_row))
        square = fx * fx + fy
        shifts = []
        for branch in range(2):
            target = squares[branch] - square
            cycles = depth_step * jnp.sqrt(jnp.abs(target))
            cosine, sine = cis(cycles)
            live = target >= 0
            shifts.append(
                (
                    jnp.where(live, cosine, jnp.exp(-two_pi * cycles)),
                    jnp.where(live, sine, 0.0),
                )
            )
        return shifts

    return at


def propagator_kernel(place, freqs, ref_slow, *tables):
    for level, table in enumerate(tables):
        at = propagators(level, place, freqs, ref_slow)

        def step(c, carry, at=at, table=table):
            here = block_rows(c)
            second_half = pl.ds(pl.multiple_of(inner + c * sub, sub), sub)
            for k in range(outer // 2):
                columns = slice(k * inner, (k + 1) * inner)
                for branch, factor in enumerate(at(c, k)):
                    table[branch, here, columns] = factor[0]
                    table[branch, second_half, columns] = factor[1]
            return carry

        lax.fori_loop(0, inner // sub, step, 0)


def weigh_kernel(first_level, place, freqs, ref_slow, *refs):
    tiles = refs[:ring]
    for n, weights in enumerate(refs[ring:]):
        weigh(first_level + n, first_level, place, freqs, ref_slow, tiles, weights)


def slab_rows(a, top, c):
    return ((a // 4 * 2 + top) * 4 + a % 4) * rows + c * sub


def plane_chunk(a, top, c):
    return c // 2 * 8 + a % 4 * 2 + top, a // 4 * quarter + c % 2 * sub


def plane_rows(a, top, c):
    chunk, row = plane_chunk(a, top, c)
    return chunk * rows + row


def shift_kernel(rows_of, arrived, table, there_matrices, back_matrices, turns, out, spectrum, *scratch):
    forward_x_kernel(rows_of, arrived, there_matrices, turns, spectrum, scratch[1])
    back_x_kernel(spectrum, table, back_matrices, turns, out, *scratch)


def forward_x_kernel(rows_of, arrived, there_matrices, turns, spectrum, lane_turn):
    fill_lane_turns(lane_turn)
    lane = lax.broadcasted_iota(jnp.int32, (sub, inner), 1)
    low_lanes = lane < half
    groups = outer // 2
    steps = inner // sub

    def there(top, c, carry):
        position = top * half + c * sub
        here = pl.ds(pl.multiple_of(position, sub), sub)
        second_half = pl.ds(pl.multiple_of(inner + position, sub), sub)
        values = []
        for a in range(groups):
            first = arrived[pl.ds(pl.multiple_of(rows_of(a, top, c), sub), sub), :]
            second = arrived[pl.ds(pl.multiple_of(rows_of(a + groups, top, c), sub), sub), :]
            total, differ = first + second, first - second
            value = (
                jnp.where(low_lanes, total, pltpu.roll(differ, half, 1)),
                jnp.where(low_lanes, pltpu.roll(total, half, 1), differ),
            )
            turn = (lane_turn[0, a : a + 1, :], lane_turn[1, a : a + 1, :])
            values.append(value if a == 0 else times_conj(value, turn))
        values = dft(values, -1)
        for k in range(groups):
            value = times_conj(values[k], (turns[0, k, here, :], turns[1, k, here, :]))
            columns = slice(k * inner, (k + 1) * inner)
            spectrum[here, columns] = value[0]
            spectrum[second_half, columns] = value[1]
        return carry

    for top in range(2):
        lax.fori_loop(0, half // sub, functools.partial(there, top), 0, unroll=half // sub)
    matrix = (there_matrices[0], there_matrices[1])
    for n in range(4):
        columns = slice(n * 2 * inner, (n + 1) * 2 * inner)
        spectrum[:, columns] = mix(matrix, cut(spectrum[:, columns]))


def back_x_kernel(spectrum, table, back_matrices, turns, out, shifted, lane_turn):
    fill_lane_turns(lane_turn)
    lane = lax.broadcasted_iota(jnp.int32, (sub, inner), 1)
    low_lanes = lane < half
    groups = outer // 2
    steps = inner // sub

    def propagate(c, carry):
        here = block_rows(c)
        second_half = pl.ds(pl.multiple_of(inner + c * sub, sub), sub)
        for k in range(groups):
            columns = slice(k * inner, (k + 1) * inner)
            value = (spectrum[here, columns], spectrum[second_half, columns])
            for branch in range(2):
                moved = times(value, (table[branch, here, columns], table[branch, second_half, columns]))
                shifted[branch, here, columns] = moved[0]
                shifted[branch, second_half, columns] = moved[1]
        return carry

    lax.fori_loop(0, steps, propagate, 0, unroll=4)
    matrix = (back_matrices[0], back_matrices[1])
    for branch in range(2):
        for n in range(4):
            columns = slice(n * 2 * inner, (n + 1) * 2 * inner)
            shifted[branch, :, columns] = mix(matrix, cut(shifted[branch, :, columns]))

    for top in range(2):

        def back(c, carry, top=top):
            position = top * half + c * sub
            here = pl.ds(pl.multiple_of(position, sub), sub)
            second_half = pl.ds(pl.multiple_of(inner + position, sub), sub)
            for branch in range(2):
                values = []
                for k in range(groups):
                    columns = slice(k * inner, (k + 1) * inner)
                    value = (shifted[branch, here, columns], shifted[branch, second_half, columns])
                    values.append(times(value, (turns[0, k, here, :], turns[1, k, here, :])))
                values = dft(values, 1)
                for a in range(groups):
                    value = values[a]
                    if a > 0:
                        value = times(value, (lane_turn[0, a : a + 1, :], lane_turn[1, a : a + 1, :]))
                    even = jnp.where(low_lanes, value[0], pltpu.roll(value[1], half, 1))
                    odd = jnp.where(low_lanes, pltpu.roll(value[0], half, 1), value[1])
                    for at, result in ((a, even + odd), (a + groups, even - odd)):
                        chunk, row = plane_chunk(at, top, c)
                        out[chunk, branch, pl.ds(pl.multiple_of(row, sub), sub), :] = result
            return carry

        lax.fori_loop(0, half // sub, back, 0, unroll=half // sub)


def call(kernel, shapes, scratch, scalars, operands):
    vmem = pl.BlockSpec(memory_space=pltpu.VMEM)
    smem = pl.BlockSpec(memory_space=pltpu.SMEM)
    return pl.pallas_call(
        kernel,
        out_shape=[jax.ShapeDtypeStruct(s, jnp.float32) for s in shapes],
        in_specs=[smem] * len(scalars) + [vmem] * len(operands),
        out_specs=[vmem] * len(shapes),
        scratch_shapes=[pltpu.VMEM(s, jnp.float32) for s in scratch],
        compiler_params=pltpu.CompilerParams(vmem_limit_bytes=12 * 1024 * 1024),
    )(*scalars, *operands)


def exchange(values, axes):
    return lax.all_to_all(values, axes, split_axis=0, concat_axis=0, tiled=True)


def around_z(tiles, first, last):
    axes = ("zl", "zh")
    index = [n % 2 * 4 + n // 2 for n in range(ring)]
    down = [(index[n], index[n - 1]) for n in range(ring)]
    up = [(index[n - 1], index[n]) for n in range(ring)]
    tiles = dict(tiles)
    for n in range(first, last):
        tiles[n] = lax.ppermute(tiles[n - 1], axes, down)
        if n < ring // 2:
            tiles[ring - n] = lax.ppermute(tiles[(ring + 1 - n) % ring], axes, up)
    return tiles


def shards(wavefield, freqs, velocity, ref_slow):
    zh, zl = lax.axis_index("zh"), lax.axis_index("zl")
    part = (lax.axis_index("y") * 4 + lax.axis_index("x")) * 2 + lax.axis_index("c")
    place = jnp.stack([zh, zl, part])

    fy_matrix = np.stack(forward_y_matrix())
    iy_matrix = np.stack(inverse_y_matrix())
    fx_matrix = np.stack(x_matrix(-1))
    ix_matrix = np.stack(x_matrix(1))
    turn_x = np.stack(x_turns())

    plane = ("y", "x", "c")
    packed = (parts, rows, inner)
    spectrum_shape = (outer, rows, 2 * inner)
    y_turns_shape = (2, outer, inner)
    folded_shape = (2 * inner, length // 2)

    (sent,) = call(
        start_kernel,
        [(4, message, inner)],
        [spectrum_shape, y_turns_shape],
        (freqs,),
        (wavefield, velocity, fy_matrix),
    )
    sent = exchange(sent, ("y",))
    sent, cells = lax.optimization_barrier((sent[:, :cell_start], sent[:, cell_start:]))
    common = (place, cells[:, -1, 0], ref_slow)
    first_tile = cells[:, :level_rows]
    later_tile = cells[:, level_rows : depth * level_rows]
    arrived = exchange(sent.reshape(packed), ("zh", "c", "x"))
    tables = call(propagator_kernel, [(2, *folded_shape)] * depth, [], common, ())
    weights = []
    for level in range(depth):
        if level == 0:
            arrived, first_tile, later_tile = lax.optimization_barrier(
                (arrived, first_tile, later_tile)
            )
            tiles = around_z({0: first_tile}, 1, 5)
        elif level == 1:
            sent, later_tile = lax.optimization_barrier((sent, later_tile))
            tiles = around_z({0: later_tile}, 1, 3)
            arrived, tiles = lax.optimization_barrier((exchange(sent, plane), tiles))
            tiles = around_z(tiles, 3, 5)
        else:
            arrived = exchange(sent, plane)
        if level < 2:
            weights += call(
                functools.partial(weigh_kernel, level),
                [(4, outer, rows, inner)] * (depth - 1 if level else 1),
                [],
                common,
                [tiles[n] for n in range(ring)],
            )
        last = level == depth - 1
        read = plane_rows if level else slab_rows
        arrived = arrived.reshape(length, inner)
        x_scratch = [(2, *folded_shape), (2, outer // 2, inner)]
        y_scratch = [(2, outer, rows, inner), spectrum_shape, y_turns_shape]
        if last:
            (shifted,) = call(
                functools.partial(shift_kernel, read),
                [(parts, 2, rows, inner)],
                [folded_shape, *x_scratch],
                (),
                (arrived, tables[level], fx_matrix, ix_matrix, turn_x),
            )
            moved = exchange(shifted, plane)
            (sent,) = call(
                functools.partial(combine_kernel, last),
                [(4, 2, quarter, length)],
                [(2, *spectrum_shape), *y_scratch],
                (),
                (moved, weights[level], iy_matrix, fy_matrix),
            )
        else:
            (spectrum,) = call(
                functools.partial(forward_x_kernel, read),
                [folded_shape],
                x_scratch[1:],
                (),
                (arrived, fx_matrix, turn_x),
            )
            (shifted,) = call(
                back_x_kernel,
                [(parts, 2, rows, inner)],
                x_scratch,
                (),
                (spectrum, tables[level], ix_matrix, turn_x),
            )
            moved = exchange(shifted, plane)
            (fields,) = call(fields_kernel, [(2, *spectrum_shape)], [], (), (moved, iy_matrix))
            (sent,) = call(
                functools.partial(sum_kernel, last),
                [packed],
                y_scratch,
                (),
                (fields, weights[level], fy_matrix),
            )
    back = exchange(exchange(sent, ("zh",)), ("y",))
    return back.transpose(1, 0, 2, 3).reshape(2, 1, rows, length)


def solution(mesh):
    axes = ("zl", "y", "zh", "x", "c")
    return jax.shard_map(
        shards,
        mesh=Mesh(mesh.devices.reshape(2, 4, 4, 4, 2), axes),
        in_specs=(
            P(None, axes[:2], axes[2:], None),
            P(axes[:2]),
            P(None, axes[2:], axes[:2]),
            P(),
        ),
        out_specs=P(None, axes[:2], axes[2:], None),
        check_vma=False,
    )
```

```python
import functools
import math

import jax
import jax.numpy as jnp
import numpy as np
from jax import lax
from jax.experimental import pallas as pl
from jax.experimental.pallas import tpu as pltpu
from jax.sharding import Mesh
from jax.sharding import PartitionSpec as P

two_pi = 2.0 * math.pi
depth_step = 2.0

length = 2048
outer = 16
inner = 128
half = 64
rows = 64
parts = 32
sub = 8
depth = 3
ring = 8
quarter = 16
level_rows = 2 * quarter
cell_start = 8 * rows
freq_start = cell_start + depth * level_rows
message = freq_start + sub


def split_bf16(matrix):
    matrix = np.asarray(matrix, np.float32)
    high = matrix.astype(jnp.bfloat16)
    low = (matrix - high.astype(np.float32)).astype(jnp.bfloat16)
    return high, low


def dft_inner(sign):
    index = np.arange(inner)
    angle = sign * two_pi / inner * (index[:, None] * index[None, :] % inner)
    scale = 1.0 / math.sqrt(length)
    return np.cos(angle) * scale, np.sin(angle) * scale


def packed_order():
    low = np.arange(half)
    return np.concatenate([low, inner + low, half + low, inner + half + low])


def forward_y_matrix():
    real, imag = dft_inner(-1)
    full = np.block([[real, imag], [-imag, real]])
    return split_bf16(full[:, packed_order()])


def inverse_y_matrix():
    real, imag = dft_inner(1)
    full = np.block([[real, imag], [-imag, real]])
    return split_bf16(full[packed_order(), :])


def x_matrix(sign):
    real, imag = dft_inner(sign)
    return split_bf16(np.block([[real, -imag], [imag, real]]))


def x_turns():
    upper = (np.arange(inner) >= half).astype(np.int64)
    k = 2 * np.arange(outer // 2)[:, None, None] + upper[None, None, :]
    angle = two_pi / length * (k * np.arange(inner)[None, :, None])
    return np.cos(angle).astype(np.float32), np.sin(angle).astype(np.float32)


def fit_even(function, terms):
    nodes = np.cos(np.pi * (np.arange(256) + 0.5) / 256)
    basis = np.stack([nodes ** (2 * n) for n in range(terms)], axis=1)
    solved = np.linalg.lstsq(basis, function(nodes), rcond=None)[0]
    return [float(c) for c in solved]


cos_fit = fit_even(lambda z: np.cos(np.pi * z), 9)
sin_fit = fit_even(lambda z: np.pi * np.sinc(z), 9)


def cis(cycles):
    z = 2.0 * (cycles - jnp.floor(cycles + 0.5))
    square = z * z
    cosine = cos_fit[-1]
    for c in cos_fit[-2::-1]:
        cosine = cosine * square + c
    sine = sin_fit[-1]
    for c in sin_fit[-2::-1]:
        sine = sine * square + c
    return cosine, sine * z


def fill_y_turns(turns):
    k = lax.broadcasted_iota(jnp.int32, (outer, inner), 0)
    b = lax.broadcasted_iota(jnp.int32, (outer, inner), 1)
    turns[0], turns[1] = cis((k * b).astype(jnp.float32) * (1.0 / length))


def fill_lane_turns(turns):
    a = lax.broadcasted_iota(jnp.int32, (outer // 2, inner), 0)
    lane = lax.broadcasted_iota(jnp.int32, (outer // 2, inner), 1)
    turns[0], turns[1] = cis(jnp.where(lane < half, 0, a).astype(jnp.float32) * (1.0 / outer))


def times(a, b):
    return (a[0] * b[0] - a[1] * b[1], a[0] * b[1] + a[1] * b[0])


def times_conj(a, b):
    return (a[0] * b[0] + a[1] * b[1], a[1] * b[0] - a[0] * b[1])


def plus(a, b):
    return (a[0] + b[0], a[1] + b[1])


def minus(a, b):
    return (a[0] - b[0], a[1] - b[1])


def times_root(a, power, n, sign):
    eighth = (8 * power) % (8 * n)
    real, imag = a
    if eighth % n == 0:
        step = (eighth // n) % 8
        if sign < 0:
            step = (8 - step) % 8
        if step == 0:
            return a
        if step == 2:
            return (-imag, real)
        if step == 4:
            return (-real, -imag)
        if step == 6:
            return (imag, -real)
        root = math.sqrt(0.5)
        total = (real + imag) * root
        differ = (real - imag) * root
        if step == 1:
            return (differ, total)
        if step == 3:
            return (-total, differ)
        if step == 5:
            return (-differ, -total)
        return (total, -differ)
    angle = sign * two_pi * power / n
    c, s = math.cos(angle), math.sin(angle)
    return (real * c - imag * s, real * s + imag * c)


def dft(values, sign):
    n = len(values)
    if n == 2:
        return [plus(*values), minus(*values)]
    if n == 4:
        t0, t1 = plus(values[0], values[2]), minus(values[0], values[2])
        t2, t3 = plus(values[1], values[3]), minus(values[1], values[3])
        if sign > 0:
            y1 = (t1[0] - t3[1], t1[1] + t3[0])
            y3 = (t1[0] + t3[1], t1[1] - t3[0])
        else:
            y1 = (t1[0] + t3[1], t1[1] - t3[0])
            y3 = (t1[0] - t3[1], t1[1] + t3[0])
        return [plus(t0, t2), y1, minus(t0, t2), y3]
    radix = 2 if n == 8 else 4
    m = n // radix
    inside = [dft(values[s::radix], sign) for s in range(radix)]
    out = [None] * n
    for k in range(m):
        turned = [times_root(inside[s][k], s * k, n, sign) for s in range(radix)]
        for step, value in enumerate(dft(turned, sign)):
            out[k + m * step] = value
    return out


def cut(x):
    high = x.astype(jnp.bfloat16)
    low = (x - high.astype(jnp.float32)).astype(jnp.bfloat16)
    return high, low


def product(a, b):
    return jnp.dot(a, b, preferred_element_type=jnp.float32)


def mix(a, b):
    (a_high, a_low), (b_high, b_low) = a, b
    left = jnp.concatenate([a_high, a_high, a_low], axis=1)
    right = jnp.concatenate([b_high, b_low, b_high], axis=0)
    return product(left, right)


def folded(number):
    return jnp.minimum(number, length - number).astype(jnp.float32) * (1.0 / length)


def block_rows(step):
    return pl.ds(pl.multiple_of(step * sub, sub), sub)


def forward_y(read, write, spectrum, matrices, turns):
    turn_cos, turn_sin = turns[0], turns[1]

    def step(c, carry):
        here = block_rows(c)
        values = dft([read(here, a) for a in range(outer)], -1)
        for k in range(outer):
            turn = (turn_cos[k : k + 1, :], turn_sin[k : k + 1, :])
            value = values[k] if k == 0 else times_conj(values[k], turn)
            spectrum[k, here, :inner] = value[0]
            spectrum[k, here, inner:] = value[1]
        return carry

    lax.fori_loop(0, rows // sub, step, 0)
    matrix = (matrices[0], matrices[1])
    for k in range(0, outer, 4):
        block = spectrum[k : k + 4].reshape(4 * rows, 2 * inner)
        result = mix(cut(block), matrix)
        for n in range(4):
            one = result[n * rows : (n + 1) * rows]
            write(2 * (k + n), one[:, :inner])
            write(2 * (k + n) + 1, one[:, inner:])


def fill_forward_y(matrices):
    row = lax.broadcasted_iota(jnp.int32, (2 * inner, 2 * inner), 0)
    column = lax.broadcasted_iota(jnp.int32, (2 * inner, 2 * inner), 1)
    j = column % half + half * (column // inner)
    turn = 32 * (row // inner - column // half % 2) - (row % inner) * j
    cosine, _ = cis((turn % inner).astype(jnp.float32) * (1.0 / inner))
    matrices[0], matrices[1] = cut(cosine * (1.0 / math.sqrt(length)))


def start_kernel(freqs, wavefield, velocity, out, spectrum, turns, matrices):
    fill_forward_y(matrices)
    fill_y_turns(turns)

    def read(here, a):
        columns = slice(a * inner, (a + 1) * inner)
        return wavefield[0, 0, here, columns], wavefield[1, 0, here, columns]

    def write(part, value):
        y, x, c = part // 8, part // 2 % 4, part % 2
        place = (4 * c + x) * rows
        out[y, place : place + rows, :] = value

    forward_y(read, write, spectrum, matrices, turns)
    for y in range(4):
        for level in range(depth):
            for t in range(2):
                place = cell_start + (2 * level + t) * quarter
                out[y, place : place + quarter, :] = velocity[
                    level, y * quarter : (y + 1) * quarter, t * inner : (t + 1) * inner
                ]
        out[y, freq_start:, :] = jnp.full((sub, inner), freqs[0], jnp.float32)


def combine_kernel(last, moved, weights, back_matrices, matrices, out, fields, *scratch):
    fields_kernel(moved, back_matrices, fields)
    sum_kernel(last, fields, weights, matrices, out, *scratch)


def fields_kernel(moved, back_matrices, fields):
    matrix = (back_matrices[0], back_matrices[1])
    for branch in range(2):
        for k in range(0, outer, 4):
            block = jnp.concatenate(
                [
                    jnp.concatenate([moved[2 * n, branch], moved[2 * n + 1, branch]], axis=1)
                    for n in range(k, k + 4)
                ],
                axis=0,
            )
            result = mix(cut(block), matrix)
            fields[branch, k : k + 4] = result.reshape(4, rows, 2 * inner)


def sum_kernel(last, fields, weights, matrices, out, summed, spectrum, turns):
    fill_y_turns(turns)
    turn_cos, turn_sin = turns[0], turns[1]

    def back(c, carry):
        here = block_rows(c)
        for branch in range(2):
            values = []
            for k in range(outer):
                value = (fields[branch, k, here, :inner], fields[branch, k, here, inner:])
                turn = (turn_cos[k : k + 1, :], turn_sin[k : k + 1, :])
                values.append(value if k == 0 else times(value, turn))
            values = dft(values, 1)
            for a in range(outer):
                weight = (weights[2 * branch, a, here, :], weights[2 * branch + 1, a, here, :])
                value = times(values[a], weight)
                if branch == 1:
                    value = plus(value, (summed[0, a, here, :], summed[1, a, here, :]))
                if last and branch == 1:
                    columns = slice(a * inner, (a + 1) * inner)
                    inside = pl.ds(pl.multiple_of(c % 2 * sub, sub), sub)
                    out[c // 2, 0, inside, columns] = value[0]
                    out[c // 2, 1, inside, columns] = value[1]
                else:
                    summed[0, a, here, :] = value[0]
                    summed[1, a, here, :] = value[1]
        return carry

    lax.fori_loop(0, rows // sub, back, 0)
    if last:
        return

    def read(here, a):
        return summed[0, a, here, :], summed[1, a, here, :]

    def write(part, value):
        out[part] = value

    forward_y(read, write, spectrum, matrices, turns)


def weigh(level, first_level, place, freqs, ref_slow, tiles, weights):
    def full(value):
        return jnp.full((sub, inner), value, jnp.float32)

    lower, upper = full(ref_slow[level, 0]), full(ref_slow[level, 1])
    pace = depth_step * full(freqs[place[0]])
    inverse_gap = 1.0 / (upper - lower)
    turn = cis(pace * (lower - upper))

    z = 2 * place[0] + place[1]
    for n in range(ring):
        source = (z + n) % ring
        tile = tiles[n]

        def step(c, carry, source=source, tile=tile):
            from_y = c // 2
            here = pl.ds(pl.multiple_of(source // 2 * quarter + c % 2 * sub, sub), sub)
            for t in range(2):
                first = (2 * (level - first_level) + t) * quarter + c % 2 * sub
                slowness = 1.0 / tile[from_y, pl.ds(pl.multiple_of(first, sub), sub), :]
                excess = slowness - lower
                upper_weight = jnp.clip(excess * inverse_gap, 0.0, 1.0)
                lower_weight = 1.0 - upper_weight
                phase = cis(pace * excess)
                other = times(phase, turn)
                a = 2 * (source % 2 * 4 + from_y) + t
                weights[0, a, here, :] = lower_weight * phase[0]
                weights[1, a, here, :] = lower_weight * phase[1]
                weights[2, a, here, :] = upper_weight * other[0]
                weights[3, a, here, :] = upper_weight * other[1]
            return carry

        lax.fori_loop(0, 8, step, 0, unroll=2)


def propagators(level, place, freqs, ref_slow):
    lane = lax.broadcasted_iota(jnp.int32, (sub, inner), 1)
    sub_row = lax.broadcasted_iota(jnp.int32, (sub, inner), 0)
    fy = folded(place[2] // 2 + outer * (half * (place[2] % 2) + lane % half))
    fy = fy * fy
    squares = []
    for branch in range(2):
        wave = jnp.full((sub, inner), freqs[place[0]]) * jnp.full((sub, inner), ref_slow[level, branch])
        squares.append(wave * wave)

    def at(c, k):
        fx = folded(2 * k + jnp.where(lane < half, 0, 1) + outer * (c * sub + sub_row))
        square = fx * fx + fy
        shifts = []
        for branch in range(2):
            target = squares[branch] - square
            cycles = depth_step * jnp.sqrt(jnp.abs(target))
            cosine, sine = cis(cycles)
            live = target >= 0
            shifts.append(
                (
                    jnp.where(live, cosine, jnp.exp(-two_pi * cycles)),
                    jnp.where(live, sine, 0.0),
                )
            )
        return shifts

    return at


def propagator_kernel(place, freqs, ref_slow, *tables):
    for level, table in enumerate(tables):
        at = propagators(level, place, freqs, ref_slow)

        def step(c, carry, at=at, table=table):
            here = block_rows(c)
            second_half = pl.ds(pl.multiple_of(inner + c * sub, sub), sub)
            for k in range(outer // 2):
                columns = slice(k * inner, (k + 1) * inner)
                for branch, factor in enumerate(at(c, k)):
                    table[branch, here, columns] = factor[0]
                    table[branch, second_half, columns] = factor[1]
            return carry

        lax.fori_loop(0, inner // sub, step, 0)


def weigh_kernel(first_level, place, freqs, ref_slow, *refs):
    tiles = refs[:ring]
    for n, weights in enumerate(refs[ring:]):
        weigh(first_level + n, first_level, place, freqs, ref_slow, tiles, weights)


def slab_rows(a, top, c):
    return ((a // 4 * 2 + top) * 4 + a % 4) * rows + c * sub


def plane_chunk(a, top, c):
    return c // 2 * 8 + a % 4 * 2 + top, a // 4 * quarter + c % 2 * sub


def plane_rows(a, top, c):
    chunk, row = plane_chunk(a, top, c)
    return chunk * rows + row


def shift_kernel(rows_of, arrived, table, there_matrices, back_matrices, turns, out, spectrum, *scratch):
    forward_x_kernel(rows_of, arrived, there_matrices, turns, spectrum, scratch[1])
    back_x_kernel(spectrum, table, back_matrices, turns, out, *scratch)


def forward_x_kernel(rows_of, arrived, there_matrices, turns, spectrum, lane_turn):
    fill_lane_turns(lane_turn)
    lane = lax.broadcasted_iota(jnp.int32, (sub, inner), 1)
    low_lanes = lane < half
    groups = outer // 2
    steps = inner // sub

    def there(top, c, carry):
        position = top * half + c * sub
        here = pl.ds(pl.multiple_of(position, sub), sub)
        second_half = pl.ds(pl.multiple_of(inner + position, sub), sub)
        values = []
        for a in range(groups):
            first = arrived[pl.ds(pl.multiple_of(rows_of(a, top, c), sub), sub), :]
            second = arrived[pl.ds(pl.multiple_of(rows_of(a + groups, top, c), sub), sub), :]
            total, differ = first + second, first - second
            value = (
                jnp.where(low_lanes, total, pltpu.roll(differ, half, 1)),
                jnp.where(low_lanes, pltpu.roll(total, half, 1), differ),
            )
            turn = (lane_turn[0, a : a + 1, :], lane_turn[1, a : a + 1, :])
            values.append(value if a == 0 else times_conj(value, turn))
        values = dft(values, -1)
        for k in range(groups):
            value = times_conj(values[k], (turns[0, k, here, :], turns[1, k, here, :]))
            columns = slice(k * inner, (k + 1) * inner)
            spectrum[here, columns] = value[0]
            spectrum[second_half, columns] = value[1]
        return carry

    for top in range(2):
        lax.fori_loop(0, half // sub, functools.partial(there, top), 0, unroll=half // sub)
    matrix = (there_matrices[0], there_matrices[1])
    for n in range(4):
        columns = slice(n * 2 * inner, (n + 1) * 2 * inner)
        spectrum[:, columns] = mix(matrix, cut(spectrum[:, columns]))


def back_x_kernel(spectrum, table, back_matrices, turns, out, shifted, lane_turn):
    fill_lane_turns(lane_turn)
    lane = lax.broadcasted_iota(jnp.int32, (sub, inner), 1)
    low_lanes = lane < half
    groups = outer // 2
    steps = inner // sub

    def propagate(c, carry):
        here = block_rows(c)
        second_half = pl.ds(pl.multiple_of(inner + c * sub, sub), sub)
        for k in range(groups):
            columns = slice(k * inner, (k + 1) * inner)
            value = (spectrum[here, columns], spectrum[second_half, columns])
            for branch in range(2):
                moved = times(value, (table[branch, here, columns], table[branch, second_half, columns]))
                shifted[branch, here, columns] = moved[0]
                shifted[branch, second_half, columns] = moved[1]
        return carry

    lax.fori_loop(0, steps, propagate, 0, unroll=4)
    matrix = (back_matrices[0], back_matrices[1])
    for branch in range(2):
        for n in range(4):
            columns = slice(n * 2 * inner, (n + 1) * 2 * inner)
            shifted[branch, :, columns] = mix(matrix, cut(shifted[branch, :, columns]))

    for top in range(2):

        def back(c, carry, top=top):
            position = top * half + c * sub
            here = pl.ds(pl.multiple_of(position, sub), sub)
            second_half = pl.ds(pl.multiple_of(inner + position, sub), sub)
            for branch in range(2):
                values = []
                for k in range(groups):
                    columns = slice(k * inner, (k + 1) * inner)
                    value = (shifted[branch, here, columns], shifted[branch, second_half, columns])
                    values.append(times(value, (turns[0, k, here, :], turns[1, k, here, :])))
                values = dft(values, 1)
                for a in range(groups):
                    value = values[a]
                    if a > 0:
                        value = times(value, (lane_turn[0, a : a + 1, :], lane_turn[1, a : a + 1, :]))
                    even = jnp.where(low_lanes, value[0], pltpu.roll(value[1], half, 1))
                    odd = jnp.where(low_lanes, pltpu.roll(value[0], half, 1), value[1])
                    for at, result in ((a, even + odd), (a + groups, even - odd)):
                        chunk, row = plane_chunk(at, top, c)
                        out[chunk, branch, pl.ds(pl.multiple_of(row, sub), sub), :] = result
            return carry

        lax.fori_loop(0, half // sub, back, 0, unroll=half // sub)


def call(kernel, shapes, scratch, scalars, operands):
    vmem = pl.BlockSpec(memory_space=pltpu.VMEM)
    smem = pl.BlockSpec(memory_space=pltpu.SMEM)
    return pl.pallas_call(
        kernel,
        out_shape=[jax.ShapeDtypeStruct(s, jnp.float32) for s in shapes],
        in_specs=[smem] * len(scalars) + [vmem] * len(operands),
        out_specs=[vmem] * len(shapes),
        scratch_shapes=[pltpu.VMEM(s, jnp.float32) if isinstance(s, tuple) else s for s in scratch],
        compiler_params=pltpu.CompilerParams(vmem_limit_bytes=12 * 1024 * 1024),
    )(*scalars, *operands)


def exchange(values, axes):
    return lax.all_to_all(values, axes, split_axis=0, concat_axis=0, tiled=True)


def around_z(tiles, first, last):
    axes = ("zl", "zh")
    index = [n % 2 * 4 + n // 2 for n in range(ring)]
    down = [(index[n], index[n - 1]) for n in range(ring)]
    up = [(index[n - 1], index[n]) for n in range(ring)]
    tiles = dict(tiles)
    for n in range(first, last):
        tiles[n] = lax.ppermute(tiles[n - 1], axes, down)
        if n < ring // 2:
            tiles[ring - n] = lax.ppermute(tiles[(ring + 1 - n) % ring], axes, up)
    return tiles


def shards(wavefield, freqs, velocity, ref_slow):
    zh, zl = lax.axis_index("zh"), lax.axis_index("zl")
    part = (lax.axis_index("y") * 4 + lax.axis_index("x")) * 2 + lax.axis_index("c")
    place = jnp.stack([zh, zl, part])

    fy_matrix = np.stack(forward_y_matrix())
    iy_matrix = np.stack(inverse_y_matrix())
    fx_matrix = np.stack(x_matrix(-1))
    ix_matrix = np.stack(x_matrix(1))
    turn_x = np.stack(x_turns())

    plane = ("y", "x", "c")
    packed = (parts, rows, inner)
    spectrum_shape = (outer, rows, 2 * inner)
    y_turns_shape = (2, outer, inner)
    folded_shape = (2 * inner, length // 2)

    (sent,) = call(
        start_kernel,
        [(4, message, inner)],
        [
            spectrum_shape,
            y_turns_shape,
            pltpu.VMEM((2, 2 * inner, 2 * inner), jnp.bfloat16),
        ],
        (freqs,),
        (wavefield, velocity),
    )
    sent = exchange(sent, ("y",))
    sent, cells = lax.optimization_barrier((sent[:, :cell_start], sent[:, cell_start:]))
    common = (place, cells[:, -1, 0], ref_slow)
    first_tile = cells[:, :level_rows]
    later_tile = cells[:, level_rows : depth * level_rows]
    arrived = exchange(sent.reshape(packed), ("zh", "c", "x"))
    tables = call(propagator_kernel, [(2, *folded_shape)] * depth, [], common, ())
    weights = []
    for level in range(depth):
        if level == 0:
            arrived, first_tile, later_tile = lax.optimization_barrier(
                (arrived, first_tile, later_tile)
            )
            tiles = around_z({0: first_tile}, 1, 5)
        elif level == 1:
            sent, later_tile = lax.optimization_barrier((sent, later_tile))
            tiles = around_z({0: later_tile}, 1, 3)
            arrived, tiles = lax.optimization_barrier((exchange(sent, plane), tiles))
            tiles = around_z(tiles, 3, 5)
        else:
            arrived = exchange(sent, plane)
        if level < 2:
            weights += call(
                functools.partial(weigh_kernel, level),
                [(4, outer, rows, inner)] * (depth - 1 if level else 1),
                [],
                common,
                [tiles[n] for n in range(ring)],
            )
        last = level == depth - 1
        read = plane_rows if level else slab_rows
        arrived = arrived.reshape(length, inner)
        x_scratch = [(2, *folded_shape), (2, outer // 2, inner)]
        y_scratch = [(2, outer, rows, inner), spectrum_shape, y_turns_shape]
        if last:
            (shifted,) = call(
                functools.partial(shift_kernel, read),
                [(parts, 2, rows, inner)],
                [folded_shape, *x_scratch],
                (),
                (arrived, tables[level], fx_matrix, ix_matrix, turn_x),
            )
            moved = exchange(shifted, plane)
            (sent,) = call(
                functools.partial(combine_kernel, last),
                [(4, 2, quarter, length)],
                [(2, *spectrum_shape), *y_scratch],
                (),
                (moved, weights[level], iy_matrix, fy_matrix),
            )
        else:
            (spectrum,) = call(
                functools.partial(forward_x_kernel, read),
                [folded_shape],
                x_scratch[1:],
                (),
                (arrived, fx_matrix, turn_x),
            )
            (shifted,) = call(
                back_x_kernel,
                [(parts, 2, rows, inner)],
                x_scratch,
                (),
                (spectrum, tables[level], ix_matrix, turn_x),
            )
            moved = exchange(shifted, plane)
            (fields,) = call(fields_kernel, [(2, *spectrum_shape)], [], (), (moved, iy_matrix))
            (sent,) = call(
                functools.partial(sum_kernel, last),
                [packed],
                y_scratch,
                (),
                (fields, weights[level], fy_matrix),
            )
    back = exchange(exchange(sent, ("zh",)), ("y",))
    return back.transpose(1, 0, 2, 3).reshape(2, 1, rows, length)


def solution(mesh):
    axes = ("zl", "y", "zh", "x", "c")
    return jax.shard_map(
        shards,
        mesh=Mesh(mesh.devices.reshape(2, 4, 4, 4, 2), axes),
        in_specs=(
            P(None, axes[:2], axes[2:], None),
            P(axes[:2]),
            P(None, axes[2:], axes[:2]),
            P(),
        ),
        out_specs=P(None, axes[:2], axes[2:], None),
        check_vma=False,
    )
```
